32 devices in a mesh: seq: 4 (over y, core), exp: 8 (over z, x).
Axes of the slice: x: 2, y: 2, z: 4, core: 2. Of those that a mesh axis runs over, the one named last changes fastest.
Arguments:
- moe_input: bfloat16 [512, 4096], P('seq', 'exp'), may hold values from -6 to 6
- out_grad: bfloat16 [512, 4096], P('seq', 'exp'), may hold values from -6 to 6
- expert_ids: int32 [512, 2], P('seq'), may hold values from 0 to 3, all different within a row; in each aligned block of 128 rows (0 to 127, 128 to 255, ...) at most 96 rows name the same one
- expert_route_weights: float32 [512, 2], P('seq'), may hold values from 0.1 to 1
- gate_weight: bfloat16 [8, 4096, 4096], P('exp', None, 'seq'), may hold values from -0.09375 to 0.09375
- up_weight: bfloat16 [8, 4096, 4096], P('exp', None, 'seq'), may hold values from -0.09375 to 0.09375
- down_weight: bfloat16 [8, 4096, 4096], P('exp', 'seq'), may hold values from -0.0625 to 0.0625
- out_weight: bfloat16 [8192, 4096], P(None, 'exp'), may hold values from -0.09375 to 0.09375
- scan_input: bfloat16 [8192, 512], P('exp', 'seq'), may hold values from -6 to 6
- delta_raw: bfloat16 [8192, 512], P('exp', 'seq'), may hold values from -1 to 512
- mixer_gate_branch: bfloat16 [8192, 512], P('exp', 'seq'), may hold values from -6 to 6
- state_input: float32 [16, 512], P(None, 'seq'), may hold values from -0.25 to 0.25
- state_output: float32 [16, 512], P(None, 'seq'), may hold values from -1.5 to 1.5
- log_rates: float32 [16, 8192], P(None, 'exp'), may hold values from -9 to -3
- skip_gain: float32 [8192], P('exp'), may hold values from 0.5 to 1.5
- block_states: float32 [4, 16, 8192], P('seq', None, 'exp'), may hold values from -6 to 6
Outputs:
- resid_grad: bfloat16 [512, 4096], P('seq', 'exp')
- probs_grad: float32 [512, 2], P('seq')
- input_grad: bfloat16 [8192, 512], P('exp', 'seq')
- delta_grad: bfloat16 [8192, 512], P('exp', 'seq')
- gate_grad: bfloat16 [8192, 512], P('exp', 'seq')
- rates_grad: float32 [16, 8192], P(None, 'exp')
- skip_grad: float32 [8192], P('exp')
The draws below stay inside these ranges and needn't reach their ends.
Inputs may be any that keep to these rules, and one draw needn't show every extreme that they name: `expert_ids`: within each aligned block of 128 rows (one sequence shard) no expert is named by more than 96 rows, and in every draw some expert is named by exactly 96 rows of some block.
All inputs are finite; a program needn't handle non-finite values.
Results may differ from the reference program's by a relative error of at most 0.0052.
Values may be sent and summed in bfloat16 or wider, within the bound.
No kernel may reach another device: no remote copies, remote signals or barrier semaphores. Data moves between devices by JAX's collectives and lax.ppermute only.
A program may use at most 192 MiB of HBM per device.

```python
import math
import jax
import jax.numpy as jnp
import numpy as np
from jax import lax

D = 4096
INNER = 8192
NSTATE = 16
TOP = 2
FFW = 8192
T_ROW = 128
EXPERTS = 4
CAP = 96
TOKEN_TOTAL = 512
N_SEQ = 4


def packet_rows(key):
    chosen = jax.random.randint(jax.random.fold_in(key, 7), (2,), 0, TOKEN_TOTAL)
    places = jnp.arange(TOKEN_TOTAL)
    flagged = (places == chosen[0]) | (places == chosen[1])
    return flagged.astype(jnp.float32)


def draw_delta_raw(key, part):
    packet_groups = packet_rows(key)
    baseline_values = jax.random.uniform(jax.random.fold_in(key, 3), (INNER, TOKEN_TOTAL), jnp.float32, -0.5, 1.5)
    return (baseline_values * (1.0 - packet_groups[None, :]) + TOKEN_TOTAL * 1.0 * packet_groups[None, :]).astype(jnp.bfloat16)


def draw_state_input(key, part):
    packet_groups = packet_rows(key)
    baseline_values = 0.05 * jnp.clip(jax.random.normal(jax.random.fold_in(key, 11), (NSTATE, TOKEN_TOTAL), jnp.float32), -5.0, 5.0)
    return baseline_values * (1.0 - packet_groups[None, :]) + baseline_values * packet_groups[None, :] / (TOKEN_TOTAL * 1.0)


def draw_log_rates(key, part):
    levels = jax.random.uniform(jax.random.fold_in(key, 5), (NSTATE, INNER), jnp.float32)
    coin_flip = jax.random.uniform(jax.random.fold_in(key, 6), (NSTATE, INNER), jnp.float32)
    fast_share = 0.5
    fast_rate = math.log(1.0 / 50.0) + levels * math.log(50.0 / 30.0)
    slow_rate = jnp.log(0.25 / (TOKEN_TOTAL * 1.0)) + levels * math.log(0.6 / 0.25)
    slow_rate = jnp.maximum(slow_rate, -9.0)
    return jnp.where(coin_flip < fast_share, fast_rate, slow_rate)


def strengthened(array, stream_key, source, target, shards_of, factor):
    owner, partner = [(jnp.arange(array.shape[axis_at]) // (array.shape[axis_at] // shards_of)).reshape([-1 if axis == axis_at else 1 for axis in range(array.ndim)]) for axis_at in (source, target)]
    chosen = jax.random.permutation(stream_key, shards_of)[partner]
    strong = (owner == chosen) | (owner == (partner + shards_of // 2) % shards_of)
    return jnp.where(strong, factor * array, array)


def block_scale(key, dims, shards, smallest, largest):
    def one(axis_at, blocks):
        steps = jax.random.uniform(jax.random.fold_in(jax.random.fold_in(key, 6), axis_at), (blocks,), jnp.float32, smallest / len(shards), largest / len(shards))
        return jnp.repeat(jnp.exp(steps), dims[axis_at] // blocks).reshape((-1,) + (1,) * (len(dims) - axis_at - 1))

    gain = one(*shards[0])
    for cut in shards[1:]:
        gain = gain * one(*cut)
    return gain


def shared_out(key, own, number, rows, number_of, top, bound, skew):
    sequence = jax.random.permutation(key, number_of)
    heavy_load, ordinary = load_shares(number_of, rows * top, bound, skew, True), load_shares(number_of, rows * top, bound, skew, False)
    places = jnp.arange(number_of)

    def named(lengths, rotation):
        used = int((lengths > 0).sum())
        fixed = max(1, used // 4)
        moved = fixed + (places - fixed + rotation * (used - fixed)) % max(1, number_of - fixed)
        return jnp.zeros((number_of,), jnp.int32).at[sequence[jnp.where(places < fixed, places, moved)]].set(jnp.asarray(lengths, jnp.int32))

    lengths = jnp.where(number % 4 == 0, named(heavy_load, number // 4), named(ordinary, number - number // 4 - 1))
    mixed = jax.random.permutation(jax.random.fold_in(own, 3), number_of)
    giver, taker = mixed[0:number_of // 2 * 2:2], mixed[1:number_of // 2 * 2:2]
    margin = jnp.minimum(lengths[giver] - 1, bound - lengths[taker]) // 2
    margin = jnp.where((giver == sequence[0]) | (taker == sequence[0]) | (lengths[taker] == 0), 0, jnp.maximum(margin, 0))
    moved = jax.random.randint(jax.random.fold_in(own, 4), (number_of // 2,), 0, 1 << 20) % (margin + 1)
    lengths = lengths.at[giver].add(-moved).at[taker].add(moved)
    labels = jnp.searchsorted(jnp.cumsum(lengths), jnp.arange(rows * top), side="right").astype(jnp.int32)
    listing = labels.reshape(top, rows).T
    listing = listing[jax.random.permutation(jax.random.fold_in(own, 1), rows)]
    rotation = jax.random.randint(jax.random.fold_in(own, 2), (rows, 1), 0, top)
    return jnp.take_along_axis(listing, (jnp.arange(top)[None, :] + rotation) % top, axis=1)


def load_shares(count, total, most, slope, full):
    portions = [(1 << 20) // math.isqrt(standing ** slope) + 1 for standing in range(1, count + 1)]
    largest = most if full else min(most, max(-(-total // count), total * portions[0] // sum(portions)))
    least = 1 if total - largest >= count - 1 else 0
    holding, rest = [largest] + [least] * (count - 1), total - largest - least * (count - 1)
    while rest > 0:
        candidates = [i for i in range(1, count) if holding[i] < largest] or [i for i in range(1, count) if holding[i] < most]
        pool, left = sum([portions[i] for i in candidates]), rest
        for i in candidates:
            more = min(most - holding[i], max(1, left * portions[i] // pool), rest)
            holding[i] = holding[i] + more
            rest = rest - more
    return np.array(holding)


def centred(own_key, extent, spread, reach, cuts=(), held_as=jnp.bfloat16):
    array = spread * jax.random.normal(own_key, extent, jnp.float32)
    if cuts:
        array = array * block_scale(own_key, extent, cuts, -0.22, 0.18)
    return jnp.clip(array, -reach, reach).astype(held_as)


def noise_with(key, extent, width, reach, shards, heavy, kind=jnp.bfloat16):
    result = width * jax.random.normal(key, extent, jnp.float32)
    if shards:
        result = result * block_scale(key, extent, shards, -0.22, 0.18)
    return jnp.clip(strengthened(result, jax.random.fold_in(key, 3), *heavy), -reach, reach).astype(kind)


def setup_inputs(seed: int = 0) -> dict:
    streams_of = jax.random.split(jax.random.key(seed), 17)
    moe_input = centred(streams_of[0], (TOKEN_TOTAL, D), 1.0, 6.0, ((0, 4), (1, 8)))
    out_grad = centred(streams_of[1], (TOKEN_TOTAL, D), 1.0, 6.0, ((0, 4), (1, 8)))
    expert_ids_keys = jax.random.split(jax.random.fold_in(streams_of[2], 1), TOKEN_TOTAL // T_ROW)
    expert_ids_turns = jax.random.permutation(jax.random.fold_in(streams_of[2], 3), TOKEN_TOTAL // T_ROW)
    expert_ids = jax.vmap(lambda own, number: shared_out(jax.random.fold_in(streams_of[2], 2), own, number, T_ROW, EXPERTS, TOP, CAP, 2))(expert_ids_keys, expert_ids_turns).reshape((TOKEN_TOTAL, TOP))
    expert_route_weights = jnp.clip(0.1 + 0.9 * jax.random.uniform(streams_of[3], (TOKEN_TOTAL, TOP), jnp.float32) ** block_scale(streams_of[3], (TOKEN_TOTAL, TOP), ((0, 4),), -0.2, 0.2), 0.1, 1.0)
    gate_weight = centred(streams_of[4], (2 * EXPERTS, D, FFW // 2), D ** -0.5, 0.09375, ((0, 8), (2, 4)))
    up_weight = centred(streams_of[5], (2 * EXPERTS, D, FFW // 2), D ** -0.5, 0.09375, ((0, 8), (2, 4)))
    down_weight = centred(streams_of[6], (2 * EXPERTS, FFW // 2, D), FFW ** -0.5, 0.0625, ((0, 8), (1, 4)))
    out_weight = noise_with(streams_of[7], (INNER, D), INNER ** -0.5, 0.09375, ((1, 8),), (1, 0, 8, 2.0))
    scan_input = centred(streams_of[8], (INNER, TOKEN_TOTAL), 1.0, 6.0, ((0, 8), (1, 4)))
    delta_raw = draw_delta_raw(jax.random.fold_in(streams_of[16], 71), 0)
    mixer_gate_branch = centred(streams_of[10], (INNER, TOKEN_TOTAL), 1.0, 6.0, ((0, 8), (1, 4)))
    state_input = draw_state_input(jax.random.fold_in(streams_of[16], 71), 0)
    state_output = centred(streams_of[12], (NSTATE, TOKEN_TOTAL), 0.25, 1.5, ((1, 4),), jnp.float32)
    log_rates = draw_log_rates(jax.random.fold_in(streams_of[16], 71), 0)
    skip_gain = jnp.clip(0.5 + 1.0 * jax.random.uniform(streams_of[14], (INNER,), jnp.float32) ** block_scale(streams_of[14], (INNER,), ((0, 8),), -0.2, 0.2), 0.5, 1.5)
    block_states = centred(streams_of[15], (N_SEQ, NSTATE, INNER), 1.0, 6.0, ((0, 4), (2, 8)), jnp.float32)
    return dict(moe_input=moe_input, out_grad=out_grad, expert_ids=expert_ids, expert_route_weights=expert_route_weights, gate_weight=gate_weight, up_weight=up_weight, down_weight=down_weight, out_weight=out_weight, scan_input=scan_input, delta_raw=delta_raw, mixer_gate_branch=mixer_gate_branch, state_input=state_input, state_output=state_output, log_rates=log_rates, skip_gain=skip_gain, block_states=block_states)


def combine_maps(former, latter):
    return (former[0] * latter[0], latter[0] * former[1] + latter[1])


def affine_scan(decays, drives):
    return lax.associative_scan(combine_maps, (decays, drives), axis=decays.ndim - 1)


def reverse_scan(decays, drives):
    carried, summed = affine_scan(jnp.flip(decays, -1), jnp.flip(drives, -1))
    return jnp.flip(carried, -1), jnp.flip(summed, -1)


def reference(moe_input, out_grad, expert_ids, expert_route_weights, gate_weight, up_weight, down_weight, out_weight, scan_input, delta_raw, mixer_gate_branch, state_input, state_output, log_rates, skip_gain, block_states):
    slices = 2 * N_SEQ
    narrow = FFW // slices
    blocks = expert_ids.reshape(N_SEQ, T_ROW * TOP)
    matches = (blocks[:, :, None] == jnp.arange(EXPERTS, dtype=jnp.int32)[None, None, :]).astype(jnp.int32)
    slot_ids = jnp.sum((jnp.cumsum(matches, axis=1) - matches) * matches, axis=2)
    shard_idx = jnp.broadcast_to(jnp.arange(N_SEQ, dtype=jnp.int32)[:, None], blocks.shape)
    owners = shard_idx * T_ROW + jnp.arange(T_ROW * TOP, dtype=jnp.int32)[None, :] // TOP
    slot_table = jnp.zeros((EXPERTS, N_SEQ, CAP), jnp.int32).at[blocks, shard_idx, slot_ids].set(owners)
    contract = (((1,), (1,)), ((), ()))

    def expert_terms(inputs):
        chosen, gate_pair, up_pair, down_pair = inputs
        gate_full = jnp.concatenate([gate_pair[0], gate_pair[1]], axis=1)
        up_full = jnp.concatenate([up_pair[0], up_pair[1]], axis=1)
        down_full = jnp.concatenate([down_pair[0], down_pair[1]], axis=0)
        row_ids = chosen.reshape(N_SEQ * CAP)
        rows_in = moe_input[row_ids]
        rows_grad = out_grad[row_ids]
        gate_pre = jnp.dot(rows_in, gate_full, preferred_element_type=jnp.float32)
        up_pre = jnp.dot(rows_in, up_full, preferred_element_type=jnp.float32)
        hidden_grad = lax.dot_general(rows_grad, down_full, contract, preferred_element_type=jnp.float32)
        gate_sig = jax.nn.sigmoid(gate_pre)
        silu_gate = gate_pre * gate_sig
        row_count = N_SEQ * CAP
        probes = jnp.sum((silu_gate * up_pre * hidden_grad).reshape(row_count, slices, narrow), axis=2)
        probe_sum = jnp.sum(probes, axis=1)
        grad_up = (hidden_grad * silu_gate).astype(jnp.bfloat16)
        grad_gate = (hidden_grad * up_pre * gate_sig * (1.0 + gate_pre * (1.0 - gate_sig))).astype(jnp.bfloat16)
        split_gate = grad_gate.astype(jnp.float32).reshape(row_count, slices, narrow)
        split_up = grad_up.astype(jnp.float32).reshape(row_count, slices, narrow)
        gate_cols = gate_full.astype(jnp.float32).reshape(D, slices, narrow)
        up_cols = up_full.astype(jnp.float32).reshape(D, slices, narrow)
        slice_terms = jnp.einsum("mqh,dqh->qmd", split_gate, gate_cols, precision=lax.Precision.HIGHEST)
        slice_terms = slice_terms + jnp.einsum("mqh,dqh->qmd", split_up, up_cols, precision=lax.Precision.HIGHEST)
        route_sum = jnp.sum(slice_terms, axis=0)
        return route_sum.reshape(N_SEQ, CAP, D), probe_sum.reshape(N_SEQ, CAP)

    route_grads, probe_grads = lax.map(expert_terms, (slot_table, gate_weight.reshape(EXPERTS, 2, D, FFW // 2), up_weight.reshape(EXPERTS, 2, D, FFW // 2), down_weight.reshape(EXPERTS, 2, FFW // 2, D)))
    route_grad = route_grads[blocks, shard_idx, slot_ids].reshape(TOKEN_TOTAL, TOP, D)
    probs_grad = probe_grads[blocks, shard_idx, slot_ids].reshape(TOKEN_TOTAL, TOP)
    resid_grad = (out_grad.astype(jnp.float32) + jnp.sum(expert_route_weights[:, :, None] * route_grad, axis=1)).astype(jnp.bfloat16)
    inner_grad = jnp.dot(out_weight, resid_grad.T, preferred_element_type=jnp.float32)

    groups = 16
    group_width = INNER // groups

    def channel_group(inputs):
        u_raw, d_raw, z_raw, upstream, rates_log, skip_part, start_state = inputs
        signal = u_raw.astype(jnp.float32)
        time_step = jax.nn.softplus(d_raw.astype(jnp.float32))
        decay_rate = jnp.exp(rates_log)
        decays = jnp.exp(-time_step[None] * decay_rate[:, :, None])
        drives = time_step[None] * state_input[:, None, :] * signal[None]
        split_shape = (NSTATE, group_width, N_SEQ, T_ROW)
        carried, summed = affine_scan(decays.reshape(split_shape), drives.reshape(split_shape))
        entry = start_state[..., None]
        block_state = summed + carried * entry
        block_before = jnp.concatenate([entry, block_state[..., :-1]], axis=3)
        states = block_state.reshape(NSTATE, group_width, TOKEN_TOTAL)
        earlier = block_before.reshape(NSTATE, group_width, TOKEN_TOTAL)
        scan_out = jnp.sum(state_output[:, None, :] * states, axis=0) + skip_part[:, None] * signal
        gate_act = z_raw.astype(jnp.float32)
        gate_sig = jax.nn.sigmoid(gate_act)
        y_grad = upstream * gate_act * gate_sig
        gate_out = (upstream * scan_out * gate_sig * (1.0 + gate_act * (1.0 - gate_sig))).astype(jnp.bfloat16)
        shifted = jnp.concatenate([decays[:, :, 1:], jnp.ones((NSTATE, group_width, 1), jnp.float32)], axis=2)
        unused, adjoint = reverse_scan(shifted, state_output[:, None, :] * y_grad[None])
        input_out = (jnp.sum(adjoint * time_step[None] * state_input[:, None, :], axis=0) + skip_part[:, None] * y_grad).astype(jnp.bfloat16)
        step_grad = jnp.sum(adjoint * (state_input[:, None, :] * signal[None] - decay_rate[:, :, None] * decays * earlier), axis=0)
        delta_out = (step_grad * jax.nn.sigmoid(d_raw.astype(jnp.float32))).astype(jnp.bfloat16)
        rates_out = -decay_rate * jnp.sum(adjoint * time_step[None] * decays * earlier, axis=2)
        skip_out = jnp.sum(y_grad * signal, axis=1)
        return input_out, delta_out, gate_out, rates_out, skip_out

    group_inputs = (scan_input.reshape(groups, group_width, TOKEN_TOTAL), delta_raw.reshape(groups, group_width, TOKEN_TOTAL), mixer_gate_branch.reshape(groups, group_width, TOKEN_TOTAL), inner_grad.reshape(groups, group_width, TOKEN_TOTAL), jnp.transpose(log_rates.reshape(NSTATE, groups, group_width), (1, 0, 2)), skip_gain.reshape(groups, group_width), jnp.transpose(block_states.reshape(N_SEQ, NSTATE, groups, group_width), (2, 1, 3, 0)))
    input_grad, delta_grad, gate_grad, rates_grad, skip_grad = lax.map(channel_group, group_inputs)
    input_grad = input_grad.reshape(INNER, TOKEN_TOTAL)
    delta_grad = delta_grad.reshape(INNER, TOKEN_TOTAL)
    gate_grad = gate_grad.reshape(INNER, TOKEN_TOTAL)
    rates_grad = jnp.transpose(rates_grad, (1, 0, 2)).reshape(NSTATE, INNER)
    skip_grad = skip_grad.reshape(INNER)
    return (resid_grad, probs_grad, input_grad, delta_grad, gate_grad, rates_grad, skip_grad)
```

```python
import math

import jax
import jax.numpy as jnp
from jax import lax
from jax.experimental import pallas as pl
from jax.experimental.pallas import tpu as pltpu
from jax.sharding import PartitionSpec as P

LN2 = math.log(2.0)
LANES = 128
VMEM_LIMIT = 48 * 1024 * 1024


def to_rows(rows_ref, block, group, groups):
    rows_ref[pl.ds(group, block.shape[0], stride=groups), :] = block


def forward_kernel(
    signal_ref, delta_ref, gate_ref, inmap_ref, outmap_ref, rates_ref, skip_ref, start_ref,
    kept_ref, step_rows, signal_rows, act_ref, slope_ref, weigh_ref, total_ref,
    rate_rows, state_rows, out_rows,
):
    channels, tokens = signal_ref.shape
    count = rates_ref.shape[0]
    groups = channels // LANES
    for g in range(groups):
        part = slice(g * LANES, (g + 1) * LANES)
        to_rows(signal_rows, signal_ref[part, :].astype(jnp.float32).T, g, groups)
        to_rows(step_rows, jax.nn.softplus(delta_ref[part, :].astype(jnp.float32)).T, g, groups)
        to_rows(rate_rows, jnp.exp(rates_ref[:, part]) * (-1.0 / LN2), g, groups)
        to_rows(state_rows, start_ref[:, part], g, groups)
    skip = skip_ref[...]

    def row(ref, index):
        return ref[pl.ds(pl.multiple_of(index * groups, groups), groups), :]

    def advance(t, carry):
        states, weighed, total = carry
        step = row(step_rows, t)
        signal = row(signal_rows, t)
        drive = step * signal
        out = skip * signal
        new_states, new_weighed = [], []
        for n in range(count):
            decay = jnp.exp2(step * rate_rows[n * groups : (n + 1) * groups, :])
            kept = decay * states[n]
            kept_ref[t, n] = kept
            state = kept + inmap_ref[n, t] * drive
            out = out + outmap_ref[n, t] * state
            new_weighed.append(decay * weighed[n] + step * kept)
            new_states.append(state)
        out_rows[pl.ds(pl.multiple_of(t * groups, groups), groups), :] = out
        return (tuple(new_states), tuple(new_weighed), total + step)

    zero = jnp.zeros((groups, LANES), jnp.float32)
    first = tuple(state_rows[n * groups : (n + 1) * groups, :] for n in range(count))
    unused, weighed, total = lax.fori_loop(0, tokens, advance, (first, (zero,) * count, zero))
    for n in range(count):
        weigh_ref[n] = weighed[n]
        total_ref[n] = jnp.exp2(total * rate_rows[n * groups : (n + 1) * groups, :])
    for g in range(groups):
        part = slice(g * LANES, (g + 1) * LANES)
        scan_out = out_rows[pl.ds(g, tokens, stride=groups), :].T
        gate = gate_ref[part, :].astype(jnp.float32)
        sig = jax.nn.sigmoid(gate)
        act_ref[part, :] = gate * sig
        slope_ref[part, :] = scan_out * sig * (1.0 + gate * (1.0 - sig))


def forward_call(scan_input, delta_raw, gate_branch, state_input, state_output, log_rates, skip, start):
    channels, tokens = scan_input.shape
    count = log_rates.shape[0]
    groups = channels // LANES
    f32 = jnp.float32
    vmem = pl.BlockSpec(memory_space=pltpu.VMEM)
    smem = pl.BlockSpec(memory_space=pltpu.SMEM)
    return pl.pallas_call(
        forward_kernel,
        out_shape=(
            jax.ShapeDtypeStruct((tokens, count, groups, LANES), f32),
            jax.ShapeDtypeStruct((tokens * groups, LANES), f32),
            jax.ShapeDtypeStruct((tokens * groups, LANES), f32),
            jax.ShapeDtypeStruct((channels, tokens), f32),
            jax.ShapeDtypeStruct((channels, tokens), f32),
            jax.ShapeDtypeStruct((count, groups, LANES), f32),
            jax.ShapeDtypeStruct((count, groups, LANES), f32),
        ),
        in_specs=[vmem, vmem, vmem, smem, smem, vmem, vmem, vmem],
        out_specs=(vmem,) * 7,
        scratch_shapes=[
            pltpu.VMEM((count * groups, LANES), f32),
            pltpu.VMEM((count * groups, LANES), f32),
            pltpu.VMEM((tokens * groups, LANES), f32),
        ],
        compiler_params=pltpu.CompilerParams(vmem_limit_bytes=VMEM_LIMIT),
        cost_estimate=pl.CostEstimate(
            flops=10 * channels * tokens * count,
            bytes_accessed=6 * channels * tokens * count,
            transcendentals=channels * tokens * count,
        ),
        name="scan_forward",
    )(scan_input, delta_raw, gate_branch, state_input, state_output, log_rates, skip, start)


def local_kernel(
    inner_ref, act_ref, slope_ref, step_rows, signal_rows, kept_ref, outmap_ref, rates_ref,
    gate_out, y_rows, term_ref, moment_ref, skip_out,
    rate_rows,
):
    channels, tokens = inner_ref.shape
    count = rates_ref.shape[0]
    groups = channels // LANES
    for g in range(groups):
        part = slice(g * LANES, (g + 1) * LANES)
        inner = inner_ref[part, :]
        gate_out[part, :] = (inner * slope_ref[part, :]).astype(gate_out.dtype)
        to_rows(y_rows, (inner * act_ref[part, :]).T, g, groups)
        to_rows(rate_rows, jnp.exp(rates_ref[:, part]) * (-1.0 / LN2), g, groups)

    def row(ref, index):
        return ref[pl.ds(pl.multiple_of(index * groups, groups), groups), :]

    def advance(turn, carry):
        terms, moments, skips = carry
        t = tokens - 1 - turn
        step = row(step_rows, t)
        y_grad = row(y_rows, t)
        new_terms, new_moments = [], []
        for n in range(count):
            adjoint = outmap_ref[n, t] * y_grad + terms[n]
            new_moments.append(moments[n] + adjoint * kept_ref[t, n] * step)
            new_terms.append(
                jnp.exp2(step * rate_rows[n * groups : (n + 1) * groups, :]) * adjoint
            )
        return (tuple(new_terms), tuple(new_moments), skips + y_grad * row(signal_rows, t))

    zero = jnp.zeros((groups, LANES), jnp.float32)
    terms, moments, skips = lax.fori_loop(
        0, tokens, advance, ((zero,) * count, (zero,) * count, zero)
    )
    for n in range(count):
        term_ref[n] = terms[n]
        moment_ref[n] = moments[n]
    skip_out[...] = skips


def local_call(inner, act, slope, steps, signals, kept, state_output, log_rates):
    channels, tokens = inner.shape
    count = log_rates.shape[0]
    groups = channels // LANES
    f32 = jnp.float32
    vmem = pl.BlockSpec(memory_space=pltpu.VMEM)
    smem = pl.BlockSpec(memory_space=pltpu.SMEM)
    return pl.pallas_call(
        local_kernel,
        out_shape=(
            jax.ShapeDtypeStruct((channels, tokens), jnp.bfloat16),
            jax.ShapeDtypeStruct((tokens * groups, LANES), f32),
            jax.ShapeDtypeStruct((count, groups, LANES), f32),
            jax.ShapeDtypeStruct((count, groups, LANES), f32),
            jax.ShapeDtypeStruct((groups, LANES), f32),
        ),
        in_specs=[vmem] * 6 + [smem, vmem],
        out_specs=(vmem,) * 5,
        scratch_shapes=[pltpu.VMEM((count * groups, LANES), f32)],
        compiler_params=pltpu.CompilerParams(vmem_limit_bytes=VMEM_LIMIT),
        cost_estimate=pl.CostEstimate(
            flops=8 * channels * tokens * count,
            bytes_accessed=5 * channels * tokens * count,
            transcendentals=channels * tokens * count,
        ),
        name="scan_local",
    )(inner, act, slope, steps, signals, kept, state_output, log_rates)


def adjoint_kernel(
    incoming_ref, y_rows, step_rows, signal_rows, kept_ref, delta_ref, inmap_ref, outmap_ref,
    rates_ref, skip_ref,
    input_out, delta_out,
    rate_rows, in_rows, slope_rows,
):
    channels, tokens = delta_ref.shape
    count = rates_ref.shape[0]
    groups = channels // LANES
    for g in range(groups):
        part = slice(g * LANES, (g + 1) * LANES)
        to_rows(rate_rows, jnp.exp(rates_ref[:, part]) * (-1.0 / LN2), g, groups)
    skip = skip_ref[...]

    def row(ref, index):
        return ref[pl.ds(pl.multiple_of(index * groups, groups), groups), :]

    def advance(turn, later):
        t = tokens - 1 - turn
        step = row(step_rows, t)
        y_grad = row(y_rows, t)
        pulled = jnp.zeros((groups, LANES), jnp.float32)
        decayed = jnp.zeros((groups, LANES), jnp.float32)
        new_later = []
        for n in range(count):
            rate = rate_rows[n * groups : (n + 1) * groups, :]
            adjoint = outmap_ref[n, t] * y_grad + later[n]
            pulled = pulled + inmap_ref[n, t] * adjoint
            decayed = decayed + adjoint * kept_ref[t, n] * rate
            new_later.append(jnp.exp2(step * rate) * adjoint)
        here = pl.ds(pl.multiple_of(t * groups, groups), groups)
        in_rows[here, :] = pulled * step + skip * y_grad
        slope_rows[here, :] = pulled * row(signal_rows, t) + decayed * LN2
        return tuple(new_later)

    lax.fori_loop(0, tokens, advance, tuple(incoming_ref[n] for n in range(count)))
    for g in range(groups):
        part = slice(g * LANES, (g + 1) * LANES)
        input_out[part, :] = in_rows[pl.ds(g, tokens, stride=groups), :].T.astype(input_out.dtype)
        sig = jax.nn.sigmoid(delta_ref[part, :].astype(jnp.float32))
        slope = slope_rows[pl.ds(g, tokens, stride=groups), :].T
        delta_out[part, :] = (slope * sig).astype(delta_out.dtype)


def adjoint_call(incoming, y_grads, steps, signals, kept, delta_raw, state_input, state_output, log_rates, skip):
    channels, tokens = delta_raw.shape
    count = log_rates.shape[0]
    groups = channels // LANES
    f32 = jnp.float32
    vmem = pl.BlockSpec(memory_space=pltpu.VMEM)
    smem = pl.BlockSpec(memory_space=pltpu.SMEM)
    return pl.pallas_call(
        adjoint_kernel,
        out_shape=(
            jax.ShapeDtypeStruct((channels, tokens), jnp.bfloat16),
            jax.ShapeDtypeStruct((channels, tokens), jnp.bfloat16),
        ),
        in_specs=[vmem] * 6 + [smem, smem, vmem, vmem],
        out_specs=(vmem,) * 2,
        scratch_shapes=[
            pltpu.VMEM((count * groups, LANES), f32),
            pltpu.VMEM((tokens * groups, LANES), f32),
            pltpu.VMEM((tokens * groups, LANES), f32),
        ],
        compiler_params=pltpu.CompilerParams(vmem_limit_bytes=VMEM_LIMIT),
        cost_estimate=pl.CostEstimate(
            flops=11 * channels * tokens * count,
            bytes_accessed=5 * channels * tokens * count,
            transcendentals=channels * tokens * count,
        ),
        name="scan_adjoint",
    )(incoming, y_grads, steps, signals, kept, delta_raw, state_input, state_output, log_rates, skip)


def later_term(term, block_decay):
    count = lax.axis_size("seq")
    ahead = []
    for distance in range(1, count):
        pairs = [(source, source - distance) for source in range(distance, count)]
        ahead.append(
            (lax.ppermute(term, "seq", pairs), lax.ppermute(block_decay, "seq", pairs))
        )
    incoming = jnp.zeros_like(term)
    for far_term, far_decay in reversed(ahead):
        incoming = far_term + far_decay * incoming
    return incoming


def expert_backward(rows_in, rows_grad, gate_slice, up_slice, down_slice):
    contract = (((1,), (1,)), ((), ()))
    gate_pre = jnp.dot(rows_in, gate_slice, preferred_element_type=jnp.float32)
    up_pre = jnp.dot(rows_in, up_slice, preferred_element_type=jnp.float32)
    hidden_grad = lax.dot_general(
        rows_grad, down_slice, contract, preferred_element_type=jnp.float32
    )
    gate_sig = jax.nn.sigmoid(gate_pre)
    silu_gate = gate_pre * gate_sig
    probes = jnp.sum(silu_gate * up_pre * hidden_grad, axis=1)
    grad_up = (hidden_grad * silu_gate).astype(jnp.bfloat16)
    grad_gate = (hidden_grad * up_pre * gate_sig * (1.0 + gate_pre * (1.0 - gate_sig))).astype(
        jnp.bfloat16
    )
    partial_rows = lax.dot_general(
        grad_gate, gate_slice, contract, preferred_element_type=jnp.float32
    )
    partial_rows = partial_rows + lax.dot_general(
        grad_up, up_slice, contract, preferred_element_type=jnp.float32
    )
    return (partial_rows, probes)


def local(
    moe_input,
    out_grad,
    expert_ids,
    expert_route_weights,
    gate_weight,
    up_weight,
    down_weight,
    out_weight,
    scan_input,
    delta_raw,
    mixer_gate_branch,
    state_input,
    state_output,
    log_rates,
    skip_gain,
    block_states,
):
    seq_count = lax.axis_size("seq")
    exp_count = lax.axis_size("exp")
    row_count, feat_cols = moe_input.shape
    top_count = expert_ids.shape[1]
    experts = exp_count // 2
    capacity = 3 * top_count * row_count // (2 * experts)
    channels = scan_input.shape[0]
    groups = channels // LANES
    states = log_rates.shape[0]
    skip_rows = skip_gain.reshape(groups, LANES)
    kept, steps, signals, act, slope, weighed, block_decay = forward_call(
        scan_input, delta_raw, mixer_gate_branch, state_input, state_output, log_rates, skip_rows,
        block_states[0],
    )
    flat_ids = expert_ids.reshape(row_count * top_count)
    matches = (flat_ids[:, None] == jnp.arange(experts, dtype=jnp.int32)[None, :]).astype(jnp.int32)
    slot_ids = jnp.sum((jnp.cumsum(matches, axis=0) - matches) * matches, axis=1)
    owners = jnp.arange(row_count * top_count, dtype=jnp.int32) // top_count
    slot_table = jnp.zeros((capacity, experts), jnp.int32).at[slot_ids, flat_ids].set(owners)
    send_in = moe_input[slot_table]
    send_grad = out_grad[slot_table]

    def widen_pair(block):
        wide = jnp.broadcast_to(block[:, :, None, :], (capacity, experts, 2, feat_cols))
        return wide.reshape(capacity, exp_count, feat_cols)

    got_in, got_grad = (
        lax.all_to_all(widen_pair(send_in), "exp", split_axis=1, concat_axis=1, tiled=True),
        lax.all_to_all(widen_pair(send_grad), "exp", split_axis=1, concat_axis=1, tiled=True),
    )
    rows_in, rows_grad = (
        lax.all_gather(got_in.reshape(capacity, exp_count * feat_cols), "seq", axis=0, tiled=True),
        lax.all_gather(
            got_grad.reshape(capacity, exp_count * feat_cols), "seq", axis=0, tiled=True
        ),
    )
    partial_rows, probes = expert_backward(
        rows_in, rows_grad, gate_weight[0], up_weight[0], down_weight[0]
    )
    sum_part, sum_probe = (
        lax.psum_scatter(partial_rows, "seq", scatter_dimension=0, tiled=True),
        lax.psum_scatter(probes, "seq", scatter_dimension=0, tiled=True),
    )
    probe_wide = jnp.broadcast_to(sum_probe[:, None, None], (capacity, exp_count, 1))
    back_part, back_probe = (
        lax.all_to_all(
            sum_part.reshape(capacity, exp_count, feat_cols),
            "exp",
            split_axis=1,
            concat_axis=1,
            tiled=True,
        ),
        lax.all_to_all(probe_wide, "exp", split_axis=1, concat_axis=1, tiled=True),
    )
    route_sum = jnp.sum(back_part.reshape(capacity, experts, 2, feat_cols), axis=2)
    probe_sum = jnp.sum(back_probe.reshape(capacity, experts, 2), axis=2)
    route_grad = route_sum[slot_ids, flat_ids].reshape(row_count, top_count, feat_cols)
    probs_grad = probe_sum[slot_ids, flat_ids].reshape(row_count, top_count)
    mixture = jnp.sum(expert_route_weights[:, :, None] * route_grad, axis=1)
    resid_grad = (out_grad.astype(jnp.float32) + mixture).astype(jnp.bfloat16)
    block = out_weight
    inner_grad = lax.psum_scatter(
        lax.dot_general(
            block, resid_grad, (((1,), (1,)), ((), ())), preferred_element_type=jnp.float32
        ),
        "exp",
        scatter_dimension=0,
        tiled=True,
    )
    gate_grad, y_grads, term, moment, skip_part = local_call(
        inner_grad, act, slope, steps, signals, kept, state_output, log_rates
    )
    incoming = later_term(term, block_decay)
    input_grad, delta_grad = adjoint_call(
        incoming, y_grads, steps, signals, kept, delta_raw, state_input, state_output, log_rates,
        skip_rows,
    )
    moment = moment + weighed * incoming
    rate_part = -jnp.exp(log_rates) * moment.reshape(states, channels)
    rates_grad, skip_grad = lax.psum((rate_part, skip_part.reshape(channels)), "seq")
    return (resid_grad, probs_grad, input_grad, delta_grad, gate_grad, rates_grad, skip_grad)


def solution(mesh):
    in_specs = (
        P("seq", "exp"),
        P("seq", "exp"),
        P("seq", None),
        P("seq", None),
        P("exp", None, "seq"),
        P("exp", None, "seq"),
        P("exp", "seq", None),
        P(None, "exp"),
        P("exp", "seq"),
        P("exp", "seq"),
        P("exp", "seq"),
        P(None, "seq"),
        P(None, "seq"),
        P(None, "exp"),
        P("exp"),
        P("seq", None, "exp"),
    )
    out_specs = (
        P("seq", "exp"),
        P("seq", None),
        P("exp", "seq"),
        P("exp", "seq"),
        P("exp", "seq"),
        P(None, "exp"),
        P("exp"),
    )
    return jax.shard_map(local, mesh=mesh, in_specs=in_specs, out_specs=out_specs, check_vma=False)
```

```python
import functools
import math

import jax
import jax.numpy as jnp
import numpy as np
from jax import lax
from jax.experimental import pallas as pl
from jax.experimental.pallas import tpu as pltpu
from jax.sharding import Mesh, PartitionSpec as P

ORDER = (0, 1, 3, 2)
PLAN = ((3, 4),)
GROUPS = ((2, 4), (0, 2))
LAG = 1
LN2 = math.log(2.0)
LANES = 128
ROOM = 40 * 1024 * 1024


CHUNKS = 8


def whole(array):
    zeros = (0,) * len(array.shape)
    return pl.BlockSpec(array.shape, lambda *unused: zeros)


def busy(microseconds):
    return pl.CostEstimate(
        flops=int(microseconds * 1.1e9 * 3.0), bytes_accessed=0, transcendentals=0
    )


def staged_call(kernel, operands, kinds, outs, scratch, cost, name, room):
    fetched = [place for place, kind in enumerate(kinds) if kind == "in"]
    given, total = len(operands), len(outs)
    held = {"in": pltpu.HBM, "hbm": pltpu.HBM, "smem": pltpu.SMEM}

    def body(*refs):
        ins, rest = list(refs[:given]), refs[given:]
        made, rest = rest[:total], rest[total:]
        buffers, arrived = rest[: len(fetched)], rest[len(fetched)]
        copies = []
        for index, place in enumerate(fetched):
            copies.append(
                pltpu.make_async_copy(ins[place], buffers[index], arrived.at[index])
            )
            copies[-1].start()
            ins[place] = buffers[index]
        for copy in copies:
            copy.wait()
        kernel(*ins, *made, *rest[len(fetched) + 1 :])

    return pl.pallas_call(
        body,
        grid=(1,),
        out_shape=tuple(out for out, kind in outs),
        in_specs=[pl.BlockSpec(memory_space=held[kind]) for kind in kinds],
        out_specs=tuple(
            whole(out) if kind == "out" else pl.BlockSpec(memory_space=pltpu.HBM)
            for out, kind in outs
        ),
        scratch_shapes=[pltpu.VMEM(operands[place].shape, operands[place].dtype) for place in fetched]
        + [pltpu.SemaphoreType.DMA((len(fetched),))]
        + list(scratch),
        compiler_params=pltpu.CompilerParams(vmem_limit_bytes=room * 1024 * 1024),
        cost_estimate=busy(cost),
        name=name,
    )(*operands)


def to_rows(rows_ref, block, group, groups):
    rows_ref[pl.ds(group, block.shape[0], stride=groups), :] = block


def forward_kernel(
    signal_ref, delta_ref, gate_ref, inmap_ref, outmap_ref, rates_ref, skip_ref, start_ref,
    kept_ref, step_rows, signal_rows, act_ref, slope_ref, maps_ref,
    rate_rows, state_rows, out_rows, kept_rows, copied,
):
    channels, tokens = signal_ref.shape
    count = rates_ref.shape[0]
    groups = channels // LANES
    span = tokens // CHUNKS
    for g in range(groups):
        part = slice(g * LANES, (g + 1) * LANES)
        to_rows(signal_rows, signal_ref[part, :].astype(jnp.float32).T, g, groups)
        to_rows(step_rows, jax.nn.softplus(delta_ref[part, :].astype(jnp.float32)).T, g, groups)
        to_rows(rate_rows, jnp.exp(rates_ref[:, part]) * (-1.0 / LN2), g, groups)
        to_rows(state_rows, start_ref[:, part], g, groups)
    skip = skip_ref[...]

    def row(ref, index):
        return ref[pl.ds(pl.multiple_of(index * groups, groups), groups), :]

    def advance(t, carry):
        states, weighed, total = carry
        step = row(step_rows, t)
        signal = row(signal_rows, t)
        drive = step * signal
        out = skip * signal
        new_states, new_weighed = [], []
        for n in range(count):
            decay = jnp.exp2(step * rate_rows[n * groups : (n + 1) * groups, :])
            kept = decay * states[n]
            kept_rows[t, n] = kept
            state = kept + inmap_ref[n, t] * drive
            out = out + outmap_ref[n, t] * state
            new_weighed.append(decay * weighed[n] + step * kept)
            new_states.append(state)
        out_rows[pl.ds(pl.multiple_of(t * groups, groups), groups), :] = out
        return (tuple(new_states), tuple(new_weighed), total + step)

    zero = jnp.zeros((groups, LANES), jnp.float32)
    first = tuple(state_rows[n * groups : (n + 1) * groups, :] for n in range(count))
    carry = (first, (zero,) * count, zero)
    copies = []
    for chunk in range(CHUNKS):
        low = chunk * span
        carry = lax.fori_loop(low, low + span, advance, carry, unroll=4)
        part = pl.ds(low, span)
        copies.append(
            pltpu.make_async_copy(kept_rows.at[part], kept_ref.at[part], copied.at[chunk])
        )
        copies[-1].start()
    unused, weighed, total = carry
    for n in range(count):
        maps_ref[n] = jnp.exp2(total * rate_rows[n * groups : (n + 1) * groups, :])
        maps_ref[count + n] = weighed[n]
    for g in range(groups):
        part = slice(g * LANES, (g + 1) * LANES)
        scan_out = out_rows[pl.ds(g, tokens, stride=groups), :].T
        gate = gate_ref[part, :].astype(jnp.float32)
        sig = jax.nn.sigmoid(gate)
        act_ref[part, :] = gate * sig
        slope_ref[part, :] = scan_out * sig * (1.0 + gate * (1.0 - sig))
    for copy in copies:
        copy.wait()


def forward_call(scan_input, delta_raw, gate_branch, state_input, state_output, log_rates, skip, start):
    channels, tokens = scan_input.shape
    count = log_rates.shape[0]
    groups = channels // LANES
    f32 = jnp.float32
    kept = pltpu.HBM((tokens, count, groups, LANES), f32)
    rows = jax.ShapeDtypeStruct((tokens * groups, LANES), f32)
    column = jax.ShapeDtypeStruct((channels, tokens), f32)
    maps = jax.ShapeDtypeStruct((2 * count, groups, LANES), f32)
    return staged_call(
        forward_kernel,
        (scan_input, delta_raw, gate_branch, state_input, state_output, log_rates, skip, start),
        ("in", "in", "in", "smem", "smem", "in", "in", "in"),
        ((kept, "hbm"),) + tuple((out, "out") for out in (rows, rows, column, column, maps)),
        [
            pltpu.VMEM((count * groups, LANES), f32),
            pltpu.VMEM((count * groups, LANES), f32),
            pltpu.VMEM((tokens * groups, LANES), f32),
            pltpu.VMEM(kept.shape, f32),
            pltpu.SemaphoreType.DMA((CHUNKS,)),
        ],
        7,
        "scan_forward",
        50,
    )


def fetch_back(kept_ref, kept_rows, copied, span):
    copies = []
    for chunk in reversed(range(CHUNKS)):
        part = pl.ds(chunk * span, span)
        copies.append(
            pltpu.make_async_copy(kept_ref.at[part], kept_rows.at[part], copied.at[chunk])
        )
        copies[-1].start()
    return copies


def local_kernel(
    extra, act_ref, slope_ref, step_rows, signal_rows, kept_ref, outmap_ref, rates_ref, *refs
):
    *inner_refs, gate_out, y_rows, sums_ref, rate_rows, kept_rows, copied = refs[extra:]
    channels, tokens = act_ref.shape
    count = rates_ref.shape[0]
    groups = channels // LANES
    span = tokens // CHUNKS
    copies = fetch_back(kept_ref, kept_rows, copied, span)
    for g in range(groups):
        part = slice(g * LANES, (g + 1) * LANES)
        inner = sum(ref[part, :].astype(jnp.float32) for ref in inner_refs)
        gate_out[part, :] = (inner * slope_ref[part, :]).astype(gate_out.dtype)
        to_rows(y_rows, (inner * act_ref[part, :]).T, g, groups)
        to_rows(rate_rows, jnp.exp(rates_ref[:, part]) * (-1.0 / LN2), g, groups)

    def row(ref, index):
        return ref[pl.ds(pl.multiple_of(index * groups, groups), groups), :]

    def advance(turn, carry):
        terms, moments, skips = carry
        t = tokens - 1 - turn
        step = row(step_rows, t)
        y_grad = row(y_rows, t)
        new_terms, new_moments = [], []
        for n in range(count):
            adjoint = outmap_ref[n, t] * y_grad + terms[n]
            new_moments.append(moments[n] + adjoint * kept_rows[t, n] * step)
            new_terms.append(
                jnp.exp2(step * rate_rows[n * groups : (n + 1) * groups, :]) * adjoint
            )
        return (tuple(new_terms), tuple(new_moments), skips + y_grad * row(signal_rows, t))

    zero = jnp.zeros((groups, LANES), jnp.float32)
    carry = ((zero,) * count, (zero,) * count, zero)
    for turn, copy in enumerate(copies):
        copy.wait()
        carry = lax.fori_loop(turn * span, (turn + 1) * span, advance, carry, unroll=4)
    terms, moments, skips = carry
    for n in range(count):
        sums_ref[n] = terms[n]
        sums_ref[count + n] = moments[n]
    sums_ref[2 * count] = skips


def local_call(inner, joined, act, slope, steps, signals, kept, state_output, log_rates):
    channels, tokens = act.shape
    count = log_rates.shape[0]
    groups = channels // LANES
    f32 = jnp.float32
    outs = (
        jax.ShapeDtypeStruct((channels, tokens), jnp.bfloat16),
        jax.ShapeDtypeStruct((tokens * groups, LANES), f32),
        jax.ShapeDtypeStruct((2 * count + 1, groups, LANES), f32),
    )
    return staged_call(
        functools.partial(local_kernel, len(joined)),
        (act, slope, steps, signals, kept, state_output, log_rates) + tuple(joined) + tuple(inner),
        ("in", "in", "in", "in", "hbm", "smem", "in")
        + ("hbm",) * len(joined)
        + ("in",) * len(inner),
        tuple((out, "out") for out in outs),
        [
            pltpu.VMEM((count * groups, LANES), f32),
            pltpu.VMEM(kept.shape, f32),
            pltpu.SemaphoreType.DMA((CHUNKS,)),
        ],
        6,
        "scan_local",
        50,
    )


def adjoint_kernel(
    incoming_ref, y_rows, step_rows, signal_rows, kept_ref, delta_ref, inmap_ref, outmap_ref,
    rates_ref, skip_ref,
    input_out, delta_out,
    rate_rows, in_rows, slope_rows, kept_rows, copied,
):
    channels, tokens = delta_ref.shape
    count = rates_ref.shape[0]
    groups = channels // LANES
    span = tokens // CHUNKS
    copies = fetch_back(kept_ref, kept_rows, copied, span)
    for g in range(groups):
        part = slice(g * LANES, (g + 1) * LANES)
        to_rows(rate_rows, jnp.exp(rates_ref[:, part]) * (-1.0 / LN2), g, groups)
    skip = skip_ref[...]

    def row(ref, index):
        return ref[pl.ds(pl.multiple_of(index * groups, groups), groups), :]

    def advance(turn, later):
        t = tokens - 1 - turn
        step = row(step_rows, t)
        y_grad = row(y_rows, t)
        pulled = jnp.zeros((groups, LANES), jnp.float32)
        decayed = jnp.zeros((groups, LANES), jnp.float32)
        new_later = []
        for n in range(count):
            rate = rate_rows[n * groups : (n + 1) * groups, :]
            adjoint = outmap_ref[n, t] * y_grad + later[n]
            pulled = pulled + inmap_ref[n, t] * adjoint
            decayed = decayed + adjoint * kept_rows[t, n] * rate
            new_later.append(jnp.exp2(step * rate) * adjoint)
        here = pl.ds(pl.multiple_of(t * groups, groups), groups)
        in_rows[here, :] = pulled * step + skip * y_grad
        slope_rows[here, :] = pulled * row(signal_rows, t) + decayed * LN2
        return tuple(new_later)

    later = tuple(incoming_ref[n] for n in range(count))
    for turn, copy in enumerate(copies):
        copy.wait()
        later = lax.fori_loop(turn * span, (turn + 1) * span, advance, later, unroll=4)
    for g in range(groups):
        part = slice(g * LANES, (g + 1) * LANES)
        input_out[part, :] = in_rows[pl.ds(g, tokens, stride=groups), :].T.astype(input_out.dtype)
        sig = jax.nn.sigmoid(delta_ref[part, :].astype(jnp.float32))
        slope = slope_rows[pl.ds(g, tokens, stride=groups), :].T
        delta_out[part, :] = (slope * sig).astype(delta_out.dtype)


def adjoint_call(incoming, y_grads, steps, signals, kept, delta_raw, state_input, state_output, log_rates, skip):
    channels, tokens = delta_raw.shape
    count = log_rates.shape[0]
    groups = channels // LANES
    f32 = jnp.float32
    out = jax.ShapeDtypeStruct((channels, tokens), jnp.bfloat16)
    return staged_call(
        adjoint_kernel,
        (incoming, y_grads, steps, signals, kept, delta_raw, state_input, state_output, log_rates, skip),
        ("in", "in", "in", "in", "hbm", "in", "smem", "smem", "in", "in"),
        ((out, "out"), (out, "out")),
        [
            pltpu.VMEM((count * groups, LANES), f32),
            pltpu.VMEM((tokens * groups, LANES), f32),
            pltpu.VMEM((tokens * groups, LANES), f32),
            pltpu.VMEM(kept.shape, f32),
            pltpu.SemaphoreType.DMA((CHUNKS,)),
        ],
        7,
        "scan_adjoint",
        50,
    )


def swap(value, axis, distance=1):
    count = lax.axis_size(axis)
    return lax.ppermute(value, axis, [(place, place ^ distance) for place in range(count)])


def full_spec(shape):
    return pl.BlockSpec(shape, lambda *unused: (0,) * len(shape))


def marks_rows(experts):
    return -(-(2 * experts + 2) // 8) * 8


def route_kernel(places_ref, ids_ref, gains_ref, input_ref, grad_ref, *refs):
    *outs, marks_ref, mark_rows = refs
    tokens = input_ref.shape[0]
    capacity = outs[0].shape[1]
    experts = len(outs)
    place = places_ref[3 * experts]
    wanted = lax.broadcasted_iota(jnp.int32, (experts, tokens), 0) ^ place
    first, second = ids_ref[0:1, :] == wanted, ids_ref[1:2, :] == wanted
    hits = first | second
    before = lax.broadcasted_iota(jnp.int32, (tokens, tokens), 0) < lax.broadcasted_iota(
        jnp.int32, (tokens, tokens), 1
    )
    slots = jnp.dot(
        hits.astype(jnp.float32).astype(jnp.bfloat16),
        before.astype(jnp.float32).astype(jnp.bfloat16),
        preferred_element_type=jnp.float32,
    )
    slots = jnp.where(hits, slots, -1.0)
    lines = lax.broadcasted_iota(jnp.int32, (capacity, tokens), 0).astype(jnp.float32)
    for d in range(experts):
        chosen = jnp.where(slots[d : d + 1, :] == lines, 1.0, 0.0).astype(jnp.bfloat16)
        for index, source in enumerate((input_ref, grad_ref)):
            outs[d][index] = jnp.dot(
                chosen, source[...], preferred_element_type=jnp.float32
            ).astype(jnp.bfloat16)
    mark_rows[...] = jnp.zeros_like(mark_rows)
    mark_rows[0:experts, :] = slots
    mark_rows[experts : 2 * experts, :] = jnp.where(
        first, gains_ref[0:1, :], jnp.where(second, gains_ref[1:2, :], 0.0)
    )
    mark_rows[2 * experts : 2 * experts + 2, :] = ids_ref[...].astype(jnp.float32)
    marks_ref[...] = mark_rows[...].T


def route_call(places, ids, gains, moe_input, out_grad, experts, capacity):
    tokens, feats = moe_input.shape
    out = jax.ShapeDtypeStruct((2, capacity, feats), jnp.bfloat16)
    lines = marks_rows(experts)
    marks = jax.ShapeDtypeStruct((tokens, lines), jnp.float32)
    made = staged_call(
        route_kernel,
        (places, ids.T, gains.T, moe_input, out_grad),
        ("smem", "in", "in", "in", "in"),
        ((out, "out"),) * experts + ((marks, "out"),),
        [pltpu.VMEM((lines, tokens), jnp.float32)],
        1,
        "route_rows",
        63,
    )
    return made[:-1], made[-1]


def follow(value, *after):
    anywhere = pl.BlockSpec(memory_space=pl.ANY)
    return pl.pallas_call(
        lambda *refs: None,
        out_shape=jax.ShapeDtypeStruct(value.shape, value.dtype),
        in_specs=[anywhere] * (1 + len(after)),
        out_specs=anywhere,
        input_output_aliases={0: 0},
        name="follow",
    )(value, *after)


def spread_plane(rows, crosswise):
    row_count = lax.axis_size("row")
    across = swap(rows, "half")
    beside = [swap(rows, "row", r) for r in range(1, row_count)]
    if crosswise:
        corner = [swap(across, "row", r) for r in range(1, row_count)]
    else:
        corner = [swap(part, "half") for part in beside]
    mine = [rows, across] + beside + corner
    near = swap(jnp.stack(mine[: 1 + row_count]), "core")
    return mine + [near] + [swap(part, "core") for part in corner]


def piece_of(refs, row_count, core, row, half):
    if core == 0:
        return refs[half if row == 0 else half * (row_count - 1) + 1 + row]
    if row and half:
        return refs[2 * row_count + row]
    return refs[2 * row_count].at[half if row == 0 else 1 + row]


def gather_kernel(groups, blocks, first, last, places_ref, after_ref, *refs):
    row_count = blocks // 2
    per = 3 * row_count
    pieces = refs[: groups * per]
    refs = refs[groups * per :]
    weights = refs[: groups * 3]
    refs = refs[groups * 3 :]
    if not first:
        held, refs = refs[:3], refs[3:]
    outs, (rows_ref,) = refs[:-1], refs[-1:]
    unused, capacity, feats = pieces[0].shape

    @pl.when(pl.program_id(0) == 0)
    def assemble():
        half = places_ref[places_ref.shape[0] - 1]
        for q in range(groups):
            for h in range(2):
                columns = pl.ds(pl.multiple_of((half ^ h) * feats, feats), feats)
                for b in range(blocks):
                    part = piece_of(
                        pieces[q * per : (q + 1) * per], row_count, b // row_count, b % row_count, h
                    )
                    for kind in range(2):
                        rows_ref[q, kind, b * capacity : (b + 1) * capacity, columns] = part[kind]

    if first:
        gate_pre = up_pre = hidden = 0.0
    else:
        gate_pre, up_pre, hidden = (ref[...] for ref in held)
    for q in range(groups):
        gate_ref, up_ref, down_ref = weights[q * 3 : q * 3 + 3]
        rows_in, rows_grad = rows_ref[q, 0], rows_ref[q, 1]
        gate_pre += jnp.dot(rows_in, gate_ref[...], preferred_element_type=jnp.float32)
        up_pre += jnp.dot(rows_in, up_ref[...], preferred_element_type=jnp.float32)
        hidden += lax.dot_general(
            rows_grad, down_ref[...], (((1,), (1,)), ((), ())),
            preferred_element_type=jnp.float32,
        )
    if not last:
        for ref, value in zip(outs, (gate_pre, up_pre, hidden)):
            ref[...] = value
        return
    gate_out, up_out, probe_out = outs
    sig = jax.nn.sigmoid(gate_pre)
    silu = gate_pre * sig
    up_out[...] = (hidden * silu).astype(jnp.bfloat16)
    weighted = hidden * up_pre
    gate_out[...] = (weighted * sig * (1.0 + gate_pre * (1.0 - sig))).astype(jnp.bfloat16)
    probe = weighted * silu
    folded = sum(
        probe[:, at : at + LANES] for at in range(0, probe.shape[1], LANES)
    )

    @pl.when(pl.program_id(0) == 0)
    def begin():
        probe_out[...] = folded

    @pl.when(pl.program_id(0) != 0)
    def add():
        probe_out[...] += folded


def gather_call(places, distances, after, pieces, gate_weight, up_weight, down_weight, held, last):
    groups, blocks = len(pieces), 2 * lax.axis_size("row")
    unused, capacity, feats = pieces[0][0].shape
    hidden = gate_weight.shape[2]
    width = min(256, hidden)
    rows = blocks * capacity
    first = held is None
    flat = [part for q in pieces for part in q]
    in_specs = [pl.BlockSpec(memory_space=pl.ANY)]
    in_specs += [full_spec(part.shape) for part in flat]
    weights = []
    for q in distances:
        in_specs += [
            pl.BlockSpec((None, 2 * feats, width), lambda j, at, q=q: (0, at[q], j)),
            pl.BlockSpec((None, 2 * feats, width), lambda j, at, q=q: (0, at[q], j)),
            pl.BlockSpec((None, width, 2 * feats), lambda j, at, q=q: (0, j, at[q])),
        ]
        weights += [gate_weight, up_weight, down_weight]
    column = pl.BlockSpec((rows, width), lambda j, at: (0, j))
    operands = [places, after] + flat + weights
    aliases = {}
    if not first:
        if not last:
            aliases = {len(operands) + i: i for i in range(3)}
        operands += list(held)
        in_specs += [column] * 3
    if last:
        out_shape = (
            jax.ShapeDtypeStruct((rows, hidden), jnp.bfloat16),
            jax.ShapeDtypeStruct((rows, hidden), jnp.bfloat16),
            jax.ShapeDtypeStruct((rows, LANES), jnp.float32),
        )
        out_specs = (column, column, full_spec((rows, LANES)))
    else:
        out_shape = (jax.ShapeDtypeStruct((rows, hidden), jnp.float32),) * 3
        out_specs = (column,) * 3
    return pl.pallas_call(
        functools.partial(gather_kernel, groups, blocks, first, last),
        out_shape=out_shape,
        grid_spec=pltpu.PrefetchScalarGridSpec(
            num_scalar_prefetch=1,
            grid=(hidden // width,),
            in_specs=in_specs,
            out_specs=out_specs,
            scratch_shapes=[pltpu.VMEM((groups, 2, rows, 2 * feats), jnp.bfloat16)],
        ),
        input_output_aliases=aliases,
        compiler_params=pltpu.CompilerParams(vmem_limit_bytes=ROOM),
        cost_estimate=busy(4 * groups),
        name="hidden_rows",
    )(*operands)


def return_kernel(
    blocks, places_ref, gate_ref, up_ref, gate_weight, up_weight, after_ref, keep_ref, send_ref
):
    contract = (((1,), (1,)), ((), ()))
    value = lax.dot_general(
        gate_ref[...], gate_weight[...], contract, preferred_element_type=jnp.float32
    ) + lax.dot_general(up_ref[...], up_weight[...], contract, preferred_element_type=jnp.float32)
    capacity = keep_ref.shape[1]
    for b in range(blocks):
        keep_ref[b] = value[b * capacity : (b + 1) * capacity]
        at = (blocks + b) * capacity
        send_ref[b] = value[at : at + capacity].astype(jnp.bfloat16)


def return_call(places, low, high, grad_gate, grad_up, gate_weight, up_weight, after, feats, row_count):
    rows, hidden = grad_gate.shape
    count, experts = high - low, lax.axis_size("expert")
    capacity = rows // (2 * row_count)
    every = pl.BlockSpec((rows, hidden), lambda q, h, at: (0, 0))
    weight = pl.BlockSpec((None, feats, hidden), lambda q, h, at: (0, at[experts * (1 + h) + low + q], 0))
    out = pl.BlockSpec((row_count, None, None, capacity, feats), lambda q, h, at: (0, h, q, 0, 0))
    shape = (row_count, 2, count, capacity, feats)
    return pl.pallas_call(
        functools.partial(return_kernel, row_count),
        out_shape=(
            jax.ShapeDtypeStruct(shape, jnp.float32),
            jax.ShapeDtypeStruct(shape, jnp.bfloat16),
        ),
        grid_spec=pltpu.PrefetchScalarGridSpec(
            num_scalar_prefetch=1,
            grid=(count, 2),
            in_specs=[every, every, weight, weight, pl.BlockSpec(memory_space=pl.ANY)],
            out_specs=(out, out),
        ),
        compiler_params=pltpu.CompilerParams(vmem_limit_bytes=ROOM),
        cost_estimate=busy(4 * count),
        name="route_grads",
    )(places, grad_gate, grad_up, gate_weight, up_weight, after)


def corner_swap(value, distance):
    rows = lax.axis_size("row")
    pairs = [
        (row * 2 + half, (row ^ distance) * 2 + (half ^ 1))
        for row in range(rows)
        for half in range(2)
    ]
    return lax.ppermute(value, ("row", "half"), pairs)


def sum_plane(keep, send):
    row_count = keep.shape[0]
    wide, narrow = jnp.float32, jnp.bfloat16
    paired = keep + swap(send, "core").astype(wide)
    small = paired.astype(narrow)
    parts = [swap(small[0, 1], "half")]
    for r in range(1, row_count):
        parts += [corner_swap(small[r, 1], r), swap(small[r, 0], "row", r)]
    total = paired[0, 0] + sum(part.astype(wide) for part in parts)
    return small, total.astype(narrow)


def resid_kernel(marks_ref, grad_ref, *refs):
    *parts, out_ref = refs
    tokens = grad_ref.shape[0]
    experts, capacity = len(parts), parts[0].shape[0]
    lines = lax.broadcasted_iota(jnp.int32, (tokens, capacity), 1).astype(jnp.float32)
    total = grad_ref[...].astype(jnp.float32)
    for d, part in enumerate(parts):
        chosen = jnp.where(marks_ref[:, d : d + 1] == lines, 1.0, 0.0).astype(jnp.bfloat16)
        gain = marks_ref[:, experts + d : experts + d + 1]
        total += gain * jnp.dot(chosen, part[...], preferred_element_type=jnp.float32)
    out_ref[...] = total.astype(out_ref.dtype)


def resid_call(marks, out_grad, parts):
    out = jax.ShapeDtypeStruct(out_grad.shape, jnp.bfloat16)
    return staged_call(
        resid_kernel,
        (marks, out_grad) + tuple(parts),
        ("in", "in") + ("in",) * len(parts),
        ((out, "out"),),
        [],
        2,
        "resid_rows",
        63,
    )[0]


def probe_lines_kernel(probes_ref, after_ref, out_ref):
    blocks, capacity = out_ref.shape
    for b in range(blocks):
        part = probes_ref[b * capacity : (b + 1) * capacity, :].T
        out_ref[b : b + 1, :] = jnp.sum(part, axis=0, keepdims=True)


def probe_lines_call(probes, after, blocks):
    out = jax.ShapeDtypeStruct((blocks, probes.shape[0] // blocks), jnp.float32)
    return staged_call(
        probe_lines_kernel, (probes, after), ("in", "hbm"), ((out, "out"),), [], 1, "probe_lines", 16
    )[0]


def probe_kernel(places_ref, marks_ref, table_ref, out_ref):
    experts, capacity = table_ref.shape
    tokens = marks_ref.shape[0]
    place = places_ref[3 * experts]
    lines = lax.broadcasted_iota(jnp.int32, (tokens, capacity), 1).astype(jnp.float32)
    columns = lax.broadcasted_iota(jnp.int32, (tokens, 2), 1)
    named = marks_ref[:, 2 * experts : 2 * experts + 2]
    total = jnp.zeros(columns.shape, jnp.float32)
    for d in range(experts):
        taken = jnp.where(marks_ref[:, d : d + 1] == lines, table_ref[d : d + 1, :], 0.0)
        value = jnp.sum(taken, axis=1, keepdims=True)
        total += jnp.where(named == (place ^ d).astype(jnp.float32), value, 0.0)
    out_ref[...] = total


def probe_call(places, marks, table):
    out = jax.ShapeDtypeStruct((marks.shape[0], 2), jnp.float32)
    return staged_call(
        probe_kernel, (places, marks, table), ("smem", "in", "in"), ((out, "out"),), [], 1,
        "probe_rows",
        16,
    )[0]


def project_kernel(places_ref, far_weight, own_weight, resid_ref, after_ref, far_ref, own_ref):
    for weight_ref, out_ref in ((far_weight, far_ref), (own_weight, own_ref)):
        value = lax.dot_general(
            weight_ref[...], resid_ref[...], (((1,), (1,)), ((), ())),
            preferred_element_type=jnp.float32,
        )
        out_ref[...] = value.astype(out_ref.dtype)


def project_call(places, distance, out_weight, resid, after, channels):
    tokens, feats = resid.shape
    shape = (channels, tokens)
    experts = lax.axis_size("expert")
    return pl.pallas_call(
        project_kernel,
        out_shape=(
            jax.ShapeDtypeStruct(shape, jnp.bfloat16),
            jax.ShapeDtypeStruct(shape, jnp.float32),
        ),
        grid_spec=pltpu.PrefetchScalarGridSpec(
            num_scalar_prefetch=1,
            grid=(1,),
            in_specs=[
                pl.BlockSpec((channels, feats), lambda i, at: (at[2 * experts + distance], 0)),
                pl.BlockSpec((channels, feats), lambda i, at: (at[experts + distance], 0)),
                full_spec((tokens, feats)),
                pl.BlockSpec(memory_space=pl.ANY),
            ],
            out_specs=(full_spec(shape),) * 2,
        ),
        compiler_params=pltpu.CompilerParams(vmem_limit_bytes=ROOM),
        cost_estimate=busy(2),
        name="inner_parts",
    )(places, out_weight, out_weight, resid, after)


def probe_table(lines):
    experts, rows = lax.axis_size("expert"), lax.axis_size("row")
    lines = lines.reshape(2, rows, lines.shape[1])
    lines = lines[0] + swap(lines[1], "core")
    lines = lines[0] + sum(swap(lines[r], "row", r) for r in range(1, rows))
    lines = lines + swap(lines, "half")
    return jnp.stack([lines] + [swap(lines, "expert", d) for d in range(1, experts)])


def in_order(own, other):
    first = lax.axis_index("core") == 0
    return jnp.where(first, own, other), jnp.where(first, other, own)


def join_maps(maps):
    count = maps.shape[0] // 2
    former, latter = in_order(maps, swap(maps, "core"))
    decay = former[:count] * latter[:count]
    weight = latter[count:] + former[count:] * latter[:count]
    joined = jnp.concatenate([decay, weight], axis=0)
    rows = lax.axis_size("row")
    return former, latter, [joined] + [swap(joined, "row", r) for r in range(1, rows)]


def join_sums(sums, former, latter, joined):
    count = joined[0].shape[0] // 2
    rows, row = lax.axis_size("row"), lax.axis_index("row")
    ahead, behind = in_order(sums, swap(sums, "core"))
    own_term = behind[:count]
    both = ahead + behind
    pair = jnp.concatenate(
        [
            ahead[:count] + former[:count] * own_term,
            both[count : 2 * count] + former[count:] * own_term,
            both[2 * count :],
        ],
        axis=0,
    )
    pairs = [pair] + [swap(pair, "row", r) for r in range(1, rows)]
    carried = jnp.zeros_like(own_term)
    incoming = jnp.zeros_like(own_term)
    moment = jnp.zeros_like(own_term)
    for place in reversed(range(rows)):
        maps_here, pair_here = joined[0], pair
        for r in range(1, rows):
            there = (row ^ r) == place
            maps_here = jnp.where(there, joined[r], maps_here)
            pair_here = jnp.where(there, pairs[r], pair_here)
        incoming = jnp.where(row == place, carried, incoming)
        moment = moment + pair_here[count : 2 * count] + maps_here[count:] * carried
        carried = pair_here[:count] + maps_here[:count] * carried
    skips = sum(part[2 * count] for part in pairs)
    into_first = own_term + latter[:count] * incoming
    return jnp.where(lax.axis_index("core") == 0, into_first, incoming), moment, skips


def local(
    moe_input,
    out_grad,
    expert_ids,
    expert_route_weights,
    gate_weight,
    up_weight,
    down_weight,
    out_weight,
    scan_input,
    delta_raw,
    mixer_gate_branch,
    state_input,
    state_output,
    log_rates,
    skip_gain,
    block_states,
):
    experts = lax.axis_size("expert")
    row_count = lax.axis_size("row")
    tokens, feats = moe_input.shape
    capacity = 3 * expert_ids.shape[1] * tokens // (2 * experts)
    channels = scan_input.shape[0]
    groups = channels // LANES
    states = log_rates.shape[0]
    skip_rows = skip_gain.reshape(groups, LANES)
    apart = np.arange(experts) ^ np.arange(experts)[:, None]
    table = np.zeros((experts, 2, 3 * experts + 2), np.int32)
    for half in range(2):
        table[:, half, :experts] = apart
        table[:, half, experts : 2 * experts] = 2 * apart + half
        table[:, half, 2 * experts : 3 * experts] = 2 * apart + 1 - half
        table[:, half, 3 * experts] = np.arange(experts)
        table[:, half, 3 * experts + 1] = half
    places = lax.dynamic_index_in_dim(
        jnp.asarray(table.reshape(2 * experts, -1)),
        2 * lax.axis_index("expert") + lax.axis_index("half"),
        keepdims=False,
    )

    kept, steps, signals, act, slope, maps = forward_call(
        scan_input, delta_raw, mixer_gate_branch, state_input, state_output, log_rates, skip_rows,
        block_states[0],
    )
    sent, marks = route_call(
        places, expert_ids, expert_route_weights, moe_input, out_grad, experts, capacity
    )
    got = {}
    for d in ORDER:
        got[d] = sent[d] if d == 0 else swap(sent[d], "expert", d)
        if d == 1:
            got[d] = follow(got[d], maps)
    held = None
    queue = []
    step = 0
    for index, d in enumerate(ORDER):
        queue.append((d, spread_plane(got[d], d % 2 == 0)))
        while step < len(PLAN) and PLAN[step][0] == index:
            took = PLAN[step][1]
            group, queue = queue[:took], queue[took:]
            step += 1
            held = gather_call(
                places,
                [q for q, unused in group],
                maps,
                [pieces for unused, pieces in group],
                gate_weight, up_weight, down_weight, held, step == len(PLAN),
            )
    grad_gate, grad_up, probes = held

    parts = [None] * experts
    after = [probes] * LAG
    for low, high in GROUPS:
        low, high = low * experts // 4, high * experts // 4
        keep, send = return_call(
            places, low, high, grad_gate, grad_up, gate_weight, up_weight, after[-LAG], feats,
            row_count,
        )
        small, summed = sum_plane(keep, send)
        after.append(small)
        for d in reversed(range(low, high)):
            parts[d] = summed[d - low] if d == 0 else swap(summed[d - low], "expert", d)
    resid_grad = resid_call(marks, out_grad, parts)
    lines = probe_lines_call(probes, resid_grad, 2 * row_count)
    probs_grad = probe_call(places, marks, probe_table(lines))

    inner = [None] * experts
    after = [resid_grad] * 2
    for d in reversed(range(experts)):
        far_part, own_part = project_call(
            places, d, out_weight, resid_grad, after[-2], channels
        )
        far_part = swap(far_part, "half")
        after.append(far_part)
        total = own_part + far_part.astype(jnp.float32)
        inner[d] = total if d == 0 else swap(total.astype(jnp.bfloat16), "expert", d)

    former, latter, joined = join_maps(maps)
    gate_grad, y_grads, sums = local_call(
        inner, joined, act, slope, steps, signals, kept, state_output, log_rates
    )
    incoming, moment, skips = join_sums(sums, former, latter, joined)
    input_grad, delta_grad = adjoint_call(
        incoming, y_grads, steps, signals, kept, delta_raw, state_input, state_output, log_rates,
        skip_rows,
    )
    rates_grad = -jnp.exp(log_rates) * moment.reshape(states, channels)
    skip_grad = skips.reshape(channels)
    return (resid_grad, probs_grad, input_grad, delta_grad, gate_grad, rates_grad, skip_grad)


def solution(mesh):
    seq_count, exp_count = mesh.shape["seq"], mesh.shape["exp"]
    split = Mesh(
        mesh.devices.reshape(seq_count // 2, 2, exp_count // 2, 2),
        ("row", "core", "expert", "half"),
    )
    seq, exp = ("row", "core"), ("expert", "half")
    in_specs = (
        P(seq, exp),
        P(seq, exp),
        P(seq, None),
        P(seq, None),
        P(exp, None, seq),
        P(exp, None, seq),
        P(exp, seq, None),
        P(None, exp),
        P(exp, seq),
        P(exp, seq),
        P(exp, seq),
        P(None, seq),
        P(None, seq),
        P(None, exp),
        P(exp),
        P(seq, None, exp),
    )
    out_specs = (
        P(seq, exp),
        P(seq, None),
        P(exp, seq),
        P(exp, seq),
        P(exp, seq),
        P(None, exp),
        P(exp),
    )
    return jax.shard_map(local, mesh=split, in_specs=in_specs, out_specs=out_specs, check_vma=False)
```

```python
import functools
import math

import jax
import jax.numpy as jnp
import numpy as np
from jax import lax
from jax.experimental import pallas as pl
from jax.experimental.pallas import tpu as pltpu
from jax.sharding import Mesh, PartitionSpec as P

ORDER = (0, 1, 3, 2)
PLAN = ((3, 4),)
GROUPS = ((2, 4), (0, 2))
LAG = 1
LN2 = math.log(2.0)
LANES = 128
ROOM = 44 * 1024 * 1024


CHUNKS = 8


def whole(array):
    zeros = (0,) * len(array.shape)
    return pl.BlockSpec(array.shape, lambda *unused: zeros)


def busy(microseconds):
    return pl.CostEstimate(
        flops=int(microseconds * 1.1e9 * 3.0), bytes_accessed=0, transcendentals=0
    )


def staged_call(kernel, operands, kinds, outs, scratch, cost, name, room):
    fetched = [place for place, kind in enumerate(kinds) if kind == "in"]
    given, total = len(operands), len(outs)
    held = {"in": pltpu.HBM, "hbm": pltpu.HBM, "smem": pltpu.SMEM}

    def body(*refs):
        ins, rest = list(refs[:given]), refs[given:]
        made, rest = rest[:total], rest[total:]
        buffers, arrived = rest[: len(fetched)], rest[len(fetched)]
        copies = []
        for index, place in enumerate(fetched):
            copies.append(
                pltpu.make_async_copy(ins[place], buffers[index], arrived.at[index])
            )
            copies[-1].start()
            ins[place] = buffers[index]
        for copy in copies:
            copy.wait()
        kernel(*ins, *made, *rest[len(fetched) + 1 :])

    return pl.pallas_call(
        body,
        grid=(1,),
        out_shape=tuple(out for out, kind in outs),
        in_specs=[pl.BlockSpec(memory_space=held[kind]) for kind in kinds],
        out_specs=tuple(
            whole(out) if kind == "out" else pl.BlockSpec(memory_space=pltpu.HBM)
            for out, kind in outs
        ),
        scratch_shapes=[pltpu.VMEM(operands[place].shape, operands[place].dtype) for place in fetched]
        + [pltpu.SemaphoreType.DMA((len(fetched),))]
        + list(scratch),
        compiler_params=pltpu.CompilerParams(vmem_limit_bytes=room * 1024 * 1024),
        cost_estimate=busy(cost),
        name=name,
    )(*operands)


def to_rows(rows_ref, block, group, groups):
    rows_ref[pl.ds(group, block.shape[0], stride=groups), :] = block


def forward_kernel(
    signal_ref, delta_ref, gate_ref, inmap_ref, outmap_ref, rates_ref, skip_ref, start_ref,
    kept_ref, step_rows, signal_rows, act_ref, slope_ref, maps_ref,
    rate_rows, state_rows, out_rows, kept_rows, copied,
):
    channels, tokens = signal_ref.shape
    count = rates_ref.shape[0]
    groups = channels // LANES
    span = tokens // CHUNKS
    for g in range(groups):
        part = slice(g * LANES, (g + 1) * LANES)
        to_rows(signal_rows, signal_ref[part, :].astype(jnp.float32).T, g, groups)
        to_rows(step_rows, jax.nn.softplus(delta_ref[part, :].astype(jnp.float32)).T, g, groups)
        to_rows(rate_rows, jnp.exp(rates_ref[:, part]) * (-1.0 / LN2), g, groups)
        to_rows(state_rows, start_ref[:, part], g, groups)
    skip = skip_ref[...]

    def row(ref, index):
        return ref[pl.ds(pl.multiple_of(index * groups, groups), groups), :]

    def advance(t, carry):
        states, weighed, total = carry
        step = row(step_rows, t)
        signal = row(signal_rows, t)
        drive = step * signal
        out = skip * signal
        new_states, new_weighed = [], []
        for n in range(count):
            decay = jnp.exp2(step * rate_rows[n * groups : (n + 1) * groups, :])
            kept = decay * states[n]
            paced = step * kept
            kept_rows[t, n] = paced
            state = kept + inmap_ref[n, t] * drive
            out = out + outmap_ref[n, t] * state
            new_weighed.append(decay * weighed[n] + paced)
            new_states.append(state)
        out_rows[pl.ds(pl.multiple_of(t * groups, groups), groups), :] = out
        return (tuple(new_states), tuple(new_weighed), total + step)

    zero = jnp.zeros((groups, LANES), jnp.float32)
    first = tuple(state_rows[n * groups : (n + 1) * groups, :] for n in range(count))
    carry = (first, (zero,) * count, zero)
    copies = []
    for chunk in range(CHUNKS):
        low = chunk * span
        carry = lax.fori_loop(low, low + span, advance, carry, unroll=4)
        part = pl.ds(low, span)
        copies.append(
            pltpu.make_async_copy(kept_rows.at[part], kept_ref.at[part], copied.at[chunk])
        )
        copies[-1].start()
    unused, weighed, total = carry
    for n in range(count):
        maps_ref[n] = jnp.exp2(total * rate_rows[n * groups : (n + 1) * groups, :])
        maps_ref[count + n] = weighed[n]
    for g in range(groups):
        part = slice(g * LANES, (g + 1) * LANES)
        scan_out = out_rows[pl.ds(g, tokens, stride=groups), :].T
        gate = gate_ref[part, :].astype(jnp.float32)
        sig = jax.nn.sigmoid(gate)
        act_ref[part, :] = gate * sig
        slope_ref[part, :] = scan_out * sig * (1.0 + gate * (1.0 - sig))
    for copy in copies:
        copy.wait()


def forward_call(scan_input, delta_raw, gate_branch, state_input, state_output, log_rates, skip, start):
    channels, tokens = scan_input.shape
    count = log_rates.shape[0]
    groups = channels // LANES
    f32 = jnp.float32
    kept = pltpu.HBM((tokens, count, groups, LANES), f32)
    rows = pltpu.HBM((tokens * groups, LANES), f32)
    column = pltpu.HBM((channels, tokens), f32)
    maps = jax.ShapeDtypeStruct((2 * count, groups, LANES), f32)
    return staged_call(
        forward_kernel,
        (scan_input, delta_raw, gate_branch, state_input, state_output, log_rates, skip, start),
        ("in", "in", "in", "smem", "smem", "in", "in", "in"),
        ((kept, "hbm"),) + tuple((out, "out") for out in (rows, rows, column, column, maps)),
        [
            pltpu.VMEM((count * groups, LANES), f32),
            pltpu.VMEM((count * groups, LANES), f32),
            pltpu.VMEM((tokens * groups, LANES), f32),
            pltpu.VMEM(kept.shape, f32),
            pltpu.SemaphoreType.DMA((CHUNKS,)),
        ],
        7,
        "scan_forward",
        50,
    )


def fetch_back(kept_ref, kept_rows, copied, span):
    copies = []
    for chunk in reversed(range(CHUNKS)):
        part = pl.ds(chunk * span, span)
        copies.append(
            pltpu.make_async_copy(kept_ref.at[part], kept_rows.at[part], copied.at[chunk])
        )
        copies[-1].start()
    return copies


def local_kernel(
    extra, act_ref, slope_ref, step_rows, signal_rows, kept_ref, outmap_ref, rates_ref, *refs
):
    *inner_refs, gate_out, y_rows, sums_ref, rate_rows, kept_rows, copied = refs[extra:]
    channels, tokens = act_ref.shape
    count = rates_ref.shape[0]
    groups = channels // LANES
    span = tokens // CHUNKS
    copies = fetch_back(kept_ref, kept_rows, copied, span)
    for g in range(groups):
        part = slice(g * LANES, (g + 1) * LANES)
        inner = sum(ref[part, :].astype(jnp.float32) for ref in inner_refs)
        gate_out[part, :] = (inner * slope_ref[part, :]).astype(gate_out.dtype)
        to_rows(y_rows, (inner * act_ref[part, :]).T, g, groups)
        to_rows(rate_rows, jnp.exp(rates_ref[:, part]) * (-1.0 / LN2), g, groups)

    def row(ref, index):
        return ref[pl.ds(pl.multiple_of(index * groups, groups), groups), :]

    def advance(turn, carry):
        terms, moments, skips = carry
        t = tokens - 1 - turn
        step = row(step_rows, t)
        y_grad = row(y_rows, t)
        new_terms, new_moments = [], []
        for n in range(count):
            adjoint = outmap_ref[n, t] * y_grad + terms[n]
            new_moments.append(moments[n] + adjoint * kept_rows[t, n])
            new_terms.append(
                jnp.exp2(step * rate_rows[n * groups : (n + 1) * groups, :]) * adjoint
            )
        return (tuple(new_terms), tuple(new_moments), skips + y_grad * row(signal_rows, t))

    zero = jnp.zeros((groups, LANES), jnp.float32)
    carry = ((zero,) * count, (zero,) * count, zero)
    for turn, copy in enumerate(copies):
        copy.wait()
        carry = lax.fori_loop(turn * span, (turn + 1) * span, advance, carry, unroll=4)
    terms, moments, skips = carry
    for n in range(count):
        sums_ref[n] = terms[n]
        sums_ref[count + n] = moments[n]
    sums_ref[2 * count] = skips


def local_call(inner, joined, act, slope, steps, signals, kept, state_output, log_rates):
    channels, tokens = act.shape
    count = log_rates.shape[0]
    groups = channels // LANES
    f32 = jnp.float32
    outs = (
        jax.ShapeDtypeStruct((channels, tokens), jnp.bfloat16),
        jax.ShapeDtypeStruct((tokens * groups, LANES), f32),
        jax.ShapeDtypeStruct((2 * count + 1, groups, LANES), f32),
    )
    return staged_call(
        functools.partial(local_kernel, len(joined)),
        (act, slope, steps, signals, kept, state_output, log_rates) + tuple(joined) + tuple(inner),
        ("in", "in", "in", "in", "hbm", "smem", "in")
        + ("hbm",) * len(joined)
        + ("in",) * len(inner),
        tuple((out, "out") for out in outs),
        [
            pltpu.VMEM((count * groups, LANES), f32),
            pltpu.VMEM(kept.shape, f32),
            pltpu.SemaphoreType.DMA((CHUNKS,)),
        ],
        6,
        "scan_local",
        50,
    )


def adjoint_kernel(
    incoming_ref, y_rows, step_rows, signal_rows, kept_ref, delta_ref, inmap_ref, outmap_ref,
    rates_ref, skip_ref,
    input_out, delta_out,
    rate_rows, in_rows, slope_rows, kept_rows, copied,
):
    channels, tokens = delta_ref.shape
    count = rates_ref.shape[0]
    groups = channels // LANES
    span = tokens // CHUNKS
    copies = fetch_back(kept_ref, kept_rows, copied, span)
    for g in range(groups):
        part = slice(g * LANES, (g + 1) * LANES)
        to_rows(rate_rows, jnp.exp(rates_ref[:, part]) * (-1.0 / LN2), g, groups)
    skip = skip_ref[...]

    def row(ref, index):
        return ref[pl.ds(pl.multiple_of(index * groups, groups), groups), :]

    def advance(turn, later):
        t = tokens - 1 - turn
        step = row(step_rows, t)
        y_grad = row(y_rows, t)
        pulled = jnp.zeros((groups, LANES), jnp.float32)
        decayed = jnp.zeros((groups, LANES), jnp.float32)
        new_later = []
        for n in range(count):
            rate = rate_rows[n * groups : (n + 1) * groups, :]
            adjoint = outmap_ref[n, t] * y_grad + later[n]
            pulled = pulled + inmap_ref[n, t] * adjoint
            decayed = decayed + adjoint * kept_rows[t, n] * rate
            new_later.append(jnp.exp2(step * rate) * adjoint)
        here = pl.ds(pl.multiple_of(t * groups, groups), groups)
        in_rows[here, :] = pulled * step + skip * y_grad
        slope_rows[here, :] = pulled * row(signal_rows, t) + decayed * (LN2 / step)
        return tuple(new_later)

    later = tuple(incoming_ref[n] for n in range(count))
    for turn, copy in enumerate(copies):
        copy.wait()
        later = lax.fori_loop(turn * span, (turn + 1) * span, advance, later, unroll=4)
    for g in range(groups):
        part = slice(g * LANES, (g + 1) * LANES)
        input_out[part, :] = in_rows[pl.ds(g, tokens, stride=groups), :].T.astype(input_out.dtype)
        sig = jax.nn.sigmoid(delta_ref[part, :].astype(jnp.float32))
        slope = slope_rows[pl.ds(g, tokens, stride=groups), :].T
        delta_out[part, :] = (slope * sig).astype(delta_out.dtype)


def adjoint_call(incoming, y_grads, steps, signals, kept, delta_raw, state_input, state_output, log_rates, skip):
    channels, tokens = delta_raw.shape
    count = log_rates.shape[0]
    groups = channels // LANES
    f32 = jnp.float32
    out = jax.ShapeDtypeStruct((channels, tokens), jnp.bfloat16)
    return staged_call(
        adjoint_kernel,
        (incoming, y_grads, steps, signals, kept, delta_raw, state_input, state_output, log_rates, skip),
        ("in", "in", "in", "in", "hbm", "in", "smem", "smem", "in", "in"),
        ((out, "out"), (out, "out")),
        [
            pltpu.VMEM((count * groups, LANES), f32),
            pltpu.VMEM((tokens * groups, LANES), f32),
            pltpu.VMEM((tokens * groups, LANES), f32),
            pltpu.VMEM(kept.shape, f32),
            pltpu.SemaphoreType.DMA((CHUNKS,)),
        ],
        7,
        "scan_adjoint",
        50,
    )


def swap(value, axis, distance=1):
    count = lax.axis_size(axis)
    return lax.ppermute(value, axis, [(place, place ^ distance) for place in range(count)])


def full_spec(shape):
    return pl.BlockSpec(shape, lambda *unused: (0,) * len(shape))


def marks_rows(experts):
    return -(-(2 * experts + 2) // 8) * 8


def route_kernel(low, high, places_ref, ids_ref, gains_ref, input_ref, grad_ref, *refs):
    outs = refs[: high - low]
    tokens = input_ref.shape[0]
    capacity = outs[0].shape[1]
    experts = (places_ref.shape[0] - 2) // 3
    place = places_ref[3 * experts]
    wanted = lax.broadcasted_iota(jnp.int32, (experts, tokens), 0) ^ place
    first, second = ids_ref[0:1, :] == wanted, ids_ref[1:2, :] == wanted
    hits = first | second
    before = lax.broadcasted_iota(jnp.int32, (tokens, tokens), 0) < lax.broadcasted_iota(
        jnp.int32, (tokens, tokens), 1
    )
    slots = jnp.dot(
        hits.astype(jnp.float32).astype(jnp.bfloat16),
        before.astype(jnp.float32).astype(jnp.bfloat16),
        preferred_element_type=jnp.float32,
    )
    slots = jnp.where(hits, slots, -1.0)
    lines = lax.broadcasted_iota(jnp.int32, (capacity, tokens), 0).astype(jnp.float32)
    for d in range(low, high):
        chosen = jnp.where(slots[d : d + 1, :] == lines, 1.0, 0.0).astype(jnp.bfloat16)
        for index, source in enumerate((input_ref, grad_ref)):
            outs[d - low][index] = jnp.dot(
                chosen, source[...], preferred_element_type=jnp.float32
            ).astype(jnp.bfloat16)
    if low:
        return
    marks_ref, mark_rows = refs[-2:]
    mark_rows[...] = jnp.zeros_like(mark_rows)
    mark_rows[0:experts, :] = slots
    mark_rows[experts : 2 * experts, :] = jnp.where(
        first, gains_ref[0:1, :], jnp.where(second, gains_ref[1:2, :], 0.0)
    )
    mark_rows[2 * experts : 2 * experts + 2, :] = ids_ref[...].astype(jnp.float32)
    marks_ref[...] = mark_rows[...].T


def route_call(places, ids, gains, moe_input, out_grad, experts, capacity):
    tokens, feats = moe_input.shape
    out = jax.ShapeDtypeStruct((2, capacity, feats), jnp.bfloat16)
    lines = marks_rows(experts)
    marks = jax.ShapeDtypeStruct((tokens, lines), jnp.float32)
    given = (places, ids.T, gains.T, moe_input, out_grad)
    kinds = ("smem", "in", "in", "in", "in")
    far = staged_call(
        functools.partial(route_kernel, 1, experts), given, kinds, ((out, "out"),) * (experts - 1),
        [], 1, "route_rows", 63,
    )
    own, marks = staged_call(
        lambda *refs: route_kernel(0, 1, *refs[:5], *refs[6:]),
        given + (far[0],),
        kinds + ("hbm",),
        ((out, "out"), (marks, "out")),
        [pltpu.VMEM((lines, tokens), jnp.float32)],
        1,
        "route_own",
        63,
    )
    return (own,) + tuple(far), marks


def follow(value, *after):
    anywhere = pl.BlockSpec(memory_space=pl.ANY)
    return pl.pallas_call(
        lambda *refs: None,
        out_shape=jax.ShapeDtypeStruct(value.shape, value.dtype),
        in_specs=[anywhere] * (1 + len(after)),
        out_specs=anywhere,
        input_output_aliases={0: 0},
        name="follow",
    )(value, *after)


def spread_plane(rows, crosswise):
    row_count = lax.axis_size("row")
    across = swap(rows, "half")
    beside = [swap(rows, "row", r) for r in range(1, row_count)]
    if crosswise:
        corner = [swap(across, "row", r) for r in range(1, row_count)]
    else:
        corner = [swap(part, "half") for part in beside]
    mine = [rows, across] + beside + corner
    near = swap(jnp.stack(mine[: 1 + row_count]), "core")
    return mine + [near] + [swap(part, "core") for part in corner]


def piece_of(refs, row_count, core, row, half):
    if core == 0:
        return refs[half if row == 0 else half * (row_count - 1) + 1 + row]
    if row and half:
        return refs[2 * row_count + row]
    return refs[2 * row_count].at[half if row == 0 else 1 + row]


def gather_kernel(groups, blocks, first, last, places_ref, after_ref, *refs):
    row_count = blocks // 2
    per = 3 * row_count
    pieces = refs[: groups * per]
    refs = refs[groups * per :]
    weights = refs[: groups * 3]
    refs = refs[groups * 3 :]
    if not first:
        held, refs = refs[:3], refs[3:]
    outs, (rows_ref,) = refs[:-1], refs[-1:]
    unused, capacity, feats = pieces[0].shape

    @pl.when(pl.program_id(0) == 0)
    def assemble():
        half = places_ref[places_ref.shape[0] - 1]
        for q in range(groups):
            for h in range(2):
                columns = pl.ds(pl.multiple_of((half ^ h) * feats, feats), feats)
                for b in range(blocks):
                    part = piece_of(
                        pieces[q * per : (q + 1) * per], row_count, b // row_count, b % row_count, h
                    )
                    for kind in range(2):
                        rows_ref[q, kind, b * capacity : (b + 1) * capacity, columns] = part[kind]

    if first:
        gate_pre = up_pre = hidden = 0.0
    else:
        gate_pre, up_pre, hidden = (ref[...] for ref in held)
    for q in range(groups):
        gate_ref, up_ref, down_ref = weights[q * 3 : q * 3 + 3]
        rows_in, rows_grad = rows_ref[q, 0], rows_ref[q, 1]
        gate_pre += jnp.dot(rows_in, gate_ref[...], preferred_element_type=jnp.float32)
        up_pre += jnp.dot(rows_in, up_ref[...], preferred_element_type=jnp.float32)
        hidden += lax.dot_general(
            rows_grad, down_ref[...], (((1,), (1,)), ((), ())),
            preferred_element_type=jnp.float32,
        )
    if not last:
        for ref, value in zip(outs, (gate_pre, up_pre, hidden)):
            ref[...] = value
        return
    gate_out, up_out, probe_out = outs
    sig = jax.nn.sigmoid(gate_pre)
    silu = gate_pre * sig
    up_out[...] = (hidden * silu).astype(jnp.bfloat16)
    weighted = hidden * up_pre
    gate_out[...] = (weighted * sig * (1.0 + gate_pre * (1.0 - sig))).astype(jnp.bfloat16)
    probe = weighted * silu
    folded = sum(
        probe[:, at : at + LANES] for at in range(0, probe.shape[1], LANES)
    )

    @pl.when(pl.program_id(0) == 0)
    def begin():
        probe_out[...] = folded

    @pl.when(pl.program_id(0) != 0)
    def add():
        probe_out[...] += folded


def gather_call(places, distances, after, pieces, gate_weight, up_weight, down_weight, held, last):
    groups, blocks = len(pieces), 2 * lax.axis_size("row")
    unused, capacity, feats = pieces[0][0].shape
    hidden = gate_weight.shape[2]
    width = min(256, hidden)
    rows = blocks * capacity
    first = held is None
    flat = [part for q in pieces for part in q]
    in_specs = [pl.BlockSpec(memory_space=pl.ANY)]
    in_specs += [full_spec(part.shape) for part in flat]
    weights = []
    for q in distances:
        in_specs += [
            pl.BlockSpec((None, 2 * feats, width), lambda j, at, q=q: (0, at[q], j)),
            pl.BlockSpec((None, 2 * feats, width), lambda j, at, q=q: (0, at[q], j)),
            pl.BlockSpec((None, width, 2 * feats), lambda j, at, q=q: (0, j, at[q])),
        ]
        weights += [gate_weight, up_weight, down_weight]
    column = pl.BlockSpec((rows, width), lambda j, at: (0, j))
    operands = [places, after] + flat + weights
    aliases = {}
    if not first:
        if not last:
            aliases = {len(operands) + i: i for i in range(3)}
        operands += list(held)
        in_specs += [column] * 3
    if last:
        out_shape = (
            jax.ShapeDtypeStruct((rows, hidden), jnp.bfloat16),
            jax.ShapeDtypeStruct((rows, hidden), jnp.bfloat16),
            jax.ShapeDtypeStruct((rows, LANES), jnp.float32),
        )
        out_specs = (column, column, full_spec((rows, LANES)))
    else:
        out_shape = (jax.ShapeDtypeStruct((rows, hidden), jnp.float32),) * 3
        out_specs = (column,) * 3
    return pl.pallas_call(
        functools.partial(gather_kernel, groups, blocks, first, last),
        out_shape=out_shape,
        grid_spec=pltpu.PrefetchScalarGridSpec(
            num_scalar_prefetch=1,
            grid=(hidden // width,),
            in_specs=in_specs,
            out_specs=out_specs,
            scratch_shapes=[pltpu.VMEM((groups, 2, rows, 2 * feats), jnp.bfloat16)],
        ),
        input_output_aliases=aliases,
        compiler_params=pltpu.CompilerParams(vmem_limit_bytes=ROOM),
        cost_estimate=busy(4 * groups),
        name="hidden_rows",
    )(*operands)


def return_kernel(
    blocks, places_ref, gate_ref, up_ref, gate_weight, up_weight, after_ref, keep_ref, send_ref
):
    contract = (((1,), (1,)), ((), ()))
    value = lax.dot_general(
        gate_ref[...], gate_weight[...], contract, preferred_element_type=jnp.float32
    ) + lax.dot_general(up_ref[...], up_weight[...], contract, preferred_element_type=jnp.float32)
    capacity = keep_ref.shape[1]
    for b in range(blocks):
        keep_ref[b] = value[b * capacity : (b + 1) * capacity]
        at = (blocks + b) * capacity
        send_ref[b] = value[at : at + capacity].astype(jnp.bfloat16)


def return_call(places, low, high, grad_gate, grad_up, gate_weight, up_weight, after, feats, row_count):
    rows, hidden = grad_gate.shape
    count, experts = high - low, lax.axis_size("expert")
    capacity = rows // (2 * row_count)
    every = pl.BlockSpec((rows, hidden), lambda q, h, at: (0, 0))
    weight = pl.BlockSpec((None, feats, hidden), lambda q, h, at: (0, at[experts * (1 + h) + low + q], 0))
    out = pl.BlockSpec((row_count, None, None, capacity, feats), lambda q, h, at: (0, h, q, 0, 0))
    shape = (row_count, 2, count, capacity, feats)
    return pl.pallas_call(
        functools.partial(return_kernel, row_count),
        out_shape=(
            jax.ShapeDtypeStruct(shape, jnp.float32),
            jax.ShapeDtypeStruct(shape, jnp.bfloat16),
        ),
        grid_spec=pltpu.PrefetchScalarGridSpec(
            num_scalar_prefetch=1,
            grid=(count, 2),
            in_specs=[every, every, weight, weight, pl.BlockSpec(memory_space=pl.ANY)],
            out_specs=(out, out),
        ),
        compiler_params=pltpu.CompilerParams(vmem_limit_bytes=ROOM),
        cost_estimate=busy(4 * count),
        name="route_grads",
    )(places, grad_gate, grad_up, gate_weight, up_weight, after)


def corner_swap(value, distance):
    rows = lax.axis_size("row")
    pairs = [
        (row * 2 + half, (row ^ distance) * 2 + (half ^ 1))
        for row in range(rows)
        for half in range(2)
    ]
    return lax.ppermute(value, ("row", "half"), pairs)


def sum_plane(keep, send):
    row_count = keep.shape[0]
    wide, narrow = jnp.float32, jnp.bfloat16
    paired = keep + swap(send, "core").astype(wide)
    small = paired.astype(narrow)
    parts = [swap(small[0, 1], "half")]
    for r in range(1, row_count):
        parts += [corner_swap(small[r, 1], r), swap(small[r, 0], "row", r)]
    total = paired[0, 0] + sum(part.astype(wide) for part in parts)
    return small, total.astype(narrow)


def resid_kernel(marks_ref, grad_ref, *refs):
    *parts, out_ref = refs
    tokens = grad_ref.shape[0]
    experts, capacity = len(parts), parts[0].shape[0]
    lines = lax.broadcasted_iota(jnp.int32, (tokens, capacity), 1).astype(jnp.float32)
    total = grad_ref[...].astype(jnp.float32)
    for d, part in enumerate(parts):
        chosen = jnp.where(marks_ref[:, d : d + 1] == lines, 1.0, 0.0).astype(jnp.bfloat16)
        gain = marks_ref[:, experts + d : experts + d + 1]
        total += gain * jnp.dot(chosen, part[...], preferred_element_type=jnp.float32)
    out_ref[...] = total.astype(out_ref.dtype)


def resid_call(marks, out_grad, parts):
    out = jax.ShapeDtypeStruct(out_grad.shape, jnp.bfloat16)
    return staged_call(
        resid_kernel,
        (marks, out_grad) + tuple(parts),
        ("in", "in") + ("in",) * len(parts),
        ((out, "out"),),
        [],
        2,
        "resid_rows",
        63,
    )[0]


def probe_lines_kernel(probes_ref, after_ref, out_ref):
    blocks, capacity = out_ref.shape
    for b in range(blocks):
        part = probes_ref[b * capacity : (b + 1) * capacity, :].T
        out_ref[b : b + 1, :] = jnp.sum(part, axis=0, keepdims=True)


def probe_lines_call(probes, after, blocks):
    out = jax.ShapeDtypeStruct((blocks, probes.shape[0] // blocks), jnp.float32)
    return staged_call(
        probe_lines_kernel, (probes, after), ("in", "hbm"), ((out, "out"),), [], 1, "probe_lines", 16
    )[0]


def probe_kernel(places_ref, marks_ref, table_ref, out_ref):
    experts, capacity = table_ref.shape
    tokens = marks_ref.shape[0]
    place = places_ref[3 * experts]
    lines = lax.broadcasted_iota(jnp.int32, (tokens, capacity), 1).astype(jnp.float32)
    columns = lax.broadcasted_iota(jnp.int32, (tokens, 2), 1)
    named = marks_ref[:, 2 * experts : 2 * experts + 2]
    total = jnp.zeros(columns.shape, jnp.float32)
    for d in range(experts):
        taken = jnp.where(marks_ref[:, d : d + 1] == lines, table_ref[d : d + 1, :], 0.0)
        value = jnp.sum(taken, axis=1, keepdims=True)
        total += jnp.where(named == (place ^ d).astype(jnp.float32), value, 0.0)
    out_ref[...] = total


def probe_call(places, marks, table):
    out = jax.ShapeDtypeStruct((marks.shape[0], 2), jnp.float32)
    return staged_call(
        probe_kernel, (places, marks, table), ("smem", "in", "in"), ((out, "out"),), [], 1,
        "probe_rows",
        16,
    )[0]


def project_kernel(places_ref, far_weight, own_weight, resid_ref, after_ref, far_ref, own_ref):
    for weight_ref, out_ref in ((far_weight, far_ref), (own_weight, own_ref)):
        value = lax.dot_general(
            weight_ref[...], resid_ref[...], (((1,), (1,)), ((), ())),
            preferred_element_type=jnp.float32,
        )
        out_ref[...] = value.astype(out_ref.dtype)


def project_call(places, distance, out_weight, resid, after, channels):
    tokens, feats = resid.shape
    shape = (channels, tokens)
    experts = lax.axis_size("expert")
    return pl.pallas_call(
        project_kernel,
        out_shape=(
            jax.ShapeDtypeStruct(shape, jnp.bfloat16),
            jax.ShapeDtypeStruct(shape, jnp.float32),
        ),
        grid_spec=pltpu.PrefetchScalarGridSpec(
            num_scalar_prefetch=1,
            grid=(1,),
            in_specs=[
                pl.BlockSpec((channels, feats), lambda i, at: (at[2 * experts + distance], 0)),
                pl.BlockSpec((channels, feats), lambda i, at: (at[experts + distance], 0)),
                full_spec((tokens, feats)),
                pl.BlockSpec(memory_space=pl.ANY),
            ],
            out_specs=(full_spec(shape),) * 2,
        ),
        compiler_params=pltpu.CompilerParams(vmem_limit_bytes=ROOM),
        cost_estimate=busy(2),
        name="inner_parts",
    )(places, out_weight, out_weight, resid, after)


def probe_table(lines):
    experts, rows = lax.axis_size("expert"), lax.axis_size("row")
    lines = lines.reshape(2, rows, lines.shape[1])
    lines = lines[0] + swap(lines[1], "core")
    lines = lines[0] + sum(swap(lines[r], "row", r) for r in range(1, rows))
    lines = lines + swap(lines, "half")
    return jnp.stack([lines] + [swap(lines, "expert", d) for d in range(1, experts)])


def in_order(own, other):
    first = lax.axis_index("core") == 0
    return jnp.where(first, own, other), jnp.where(first, other, own)


def join_maps(maps):
    count = maps.shape[0] // 2
    former, latter = in_order(maps, swap(maps, "core"))
    decay = former[:count] * latter[:count]
    weight = latter[count:] + former[count:] * latter[:count]
    joined = jnp.concatenate([decay, weight], axis=0)
    rows = lax.axis_size("row")
    return former, latter, [joined] + [swap(joined, "row", r) for r in range(1, rows)]


def join_sums(sums, former, latter, joined):
    count = joined[0].shape[0] // 2
    rows, row = lax.axis_size("row"), lax.axis_index("row")
    ahead, behind = in_order(sums, swap(sums, "core"))
    own_term = behind[:count]
    both = ahead + behind
    pair = jnp.concatenate(
        [
            ahead[:count] + former[:count] * own_term,
            both[count : 2 * count] + former[count:] * own_term,
            both[2 * count :],
        ],
        axis=0,
    )
    pairs = [pair] + [swap(pair, "row", r) for r in range(1, rows)]
    carried = jnp.zeros_like(own_term)
    incoming = jnp.zeros_like(own_term)
    moment = jnp.zeros_like(own_term)
    for place in reversed(range(rows)):
        maps_here, pair_here = joined[0], pair
        for r in range(1, rows):
            there = (row ^ r) == place
            maps_here = jnp.where(there, joined[r], maps_here)
            pair_here = jnp.where(there, pairs[r], pair_here)
        incoming = jnp.where(row == place, carried, incoming)
        moment = moment + pair_here[count : 2 * count] + maps_here[count:] * carried
        carried = pair_here[:count] + maps_here[:count] * carried
    skips = sum(part[2 * count] for part in pairs)
    into_first = own_term + latter[:count] * incoming
    return jnp.where(lax.axis_index("core") == 0, into_first, incoming), moment, skips


def local(
    moe_input,
    out_grad,
    expert_ids,
    expert_route_weights,
    gate_weight,
    up_weight,
    down_weight,
    out_weight,
    scan_input,
    delta_raw,
    mixer_gate_branch,
    state_input,
    state_output,
    log_rates,
    skip_gain,
    block_states,
):
    experts = lax.axis_size("expert")
    row_count = lax.axis_size("row")
    tokens, feats = moe_input.shape
    capacity = 3 * expert_ids.shape[1] * tokens // (2 * experts)
    channels = scan_input.shape[0]
    groups = channels // LANES
    states = log_rates.shape[0]
    skip_rows = skip_gain.reshape(groups, LANES)
    apart = np.arange(experts) ^ np.arange(experts)[:, None]
    table = np.zeros((experts, 2, 3 * experts + 2), np.int32)
    for half in range(2):
        table[:, half, :experts] = apart
        table[:, half, experts : 2 * experts] = 2 * apart + half
        table[:, half, 2 * experts : 3 * experts] = 2 * apart + 1 - half
        table[:, half, 3 * experts] = np.arange(experts)
        table[:, half, 3 * experts + 1] = half
    places = lax.dynamic_index_in_dim(
        jnp.asarray(table.reshape(2 * experts, -1)),
        2 * lax.axis_index("expert") + lax.axis_index("half"),
        keepdims=False,
    )

    kept, steps, signals, act, slope, maps = forward_call(
        scan_input, delta_raw, mixer_gate_branch, state_input, state_output, log_rates, skip_rows,
        block_states[0],
    )
    sent, marks = route_call(
        places, expert_ids, expert_route_weights, moe_input, out_grad, experts, capacity
    )
    got = {}
    for d in ORDER:
        got[d] = sent[d] if d == 0 else swap(sent[d], "expert", d)
        if d == 1:
            got[d] = follow(got[d], maps)
    held = None
    queue = []
    step = 0
    for index, d in enumerate(ORDER):
        queue.append((d, spread_plane(got[d], d % 2 == 0)))
        while step < len(PLAN) and PLAN[step][0] == index:
            took = PLAN[step][1]
            group, queue = queue[:took], queue[took:]
            step += 1
            held = gather_call(
                places,
                [q for q, unused in group],
                maps,
                [pieces for unused, pieces in group],
                gate_weight, up_weight, down_weight, held, step == len(PLAN),
            )
    grad_gate, grad_up, probes = held

    parts = [None] * experts
    after = [probes] * LAG
    for low, high in GROUPS:
        low, high = low * experts // 4, high * experts // 4
        keep, send = return_call(
            places, low, high, grad_gate, grad_up, gate_weight, up_weight, after[-LAG], feats,
            row_count,
        )
        small, summed = sum_plane(keep, send)
        after.append(small)
        for d in reversed(range(low, high)):
            parts[d] = summed[d - low] if d == 0 else swap(summed[d - low], "expert", d)
    resid_grad = resid_call(marks, out_grad, parts)
    lines = probe_lines_call(probes, grad_up, 2 * row_count)
    probs_grad = probe_call(places, marks, probe_table(lines))

    inner = [None] * experts
    after = resid_grad
    for d in reversed(range(experts)):
        far_part, own_part = project_call(
            places, d, out_weight, resid_grad, after, channels
        )
        after = far_part
        total = own_part + swap(far_part, "half").astype(jnp.float32)
        inner[d] = total if d == 0 else swap(total.astype(jnp.bfloat16), "expert", d)

    former, latter, joined = join_maps(maps)
    gate_grad, y_grads, sums = local_call(
        inner, joined, act, slope, steps, signals, kept, state_output, log_rates
    )
    incoming, moment, skips = join_sums(sums, former, latter, joined)
    input_grad, delta_grad = adjoint_call(
        incoming, y_grads, steps, signals, kept, delta_raw, state_input, state_output, log_rates,
        skip_rows,
    )
    rates_grad = -jnp.exp(log_rates) * moment.reshape(states, channels)
    skip_grad = skips.reshape(channels)
    return (resid_grad, probs_grad, input_grad, delta_grad, gate_grad, rates_grad, skip_grad)


def solution(mesh):
    seq_count, exp_count = mesh.shape["seq"], mesh.shape["exp"]
    split = Mesh(
        mesh.devices.reshape(seq_count // 2, 2, exp_count // 2, 2),
        ("row", "core", "expert", "half"),
    )
    seq, exp = ("row", "core"), ("expert", "half")
    in_specs = (
        P(seq, exp),
        P(seq, exp),
        P(seq, None),
        P(seq, None),
        P(exp, None, seq),
        P(exp, None, seq),
        P(exp, seq, None),
        P(None, exp),
        P(exp, seq),
        P(exp, seq),
        P(exp, seq),
        P(None, seq),
        P(None, seq),
        P(None, exp),
        P(exp),
        P(seq, None, exp),
    )
    out_specs = (
        P(seq, exp),
        P(seq, None),
        P(exp, seq),
        P(exp, seq),
        P(exp, seq),
        P(None, exp),
        P(exp),
    )
    return jax.shard_map(local, mesh=split, in_specs=in_specs, out_specs=out_specs, check_vma=False)
```

```python
import functools
import math

import jax
import jax.numpy as jnp
import numpy as np
from jax import lax
from jax.experimental import pallas as pl
from jax.experimental.pallas import tpu as pltpu
from jax.sharding import Mesh, PartitionSpec as P

ORDER = (0, 1, 3, 2)
PLAN = ((3, 4),)
GROUPS = ((2, 4), (0, 2))
LAG = 1
LN2 = math.log(2.0)
LANES = 128
ROOM = 44 * 1024 * 1024


CHUNKS = 8


def whole(array):
    zeros = (0,) * len(array.shape)
    return pl.BlockSpec(array.shape, lambda *unused: zeros)


def busy(microseconds):
    return pl.CostEstimate(
        flops=int(microseconds * 1.1e9 * 3.0), bytes_accessed=0, transcendentals=0
    )


def staged_call(kernel, operands, kinds, outs, scratch, cost, name, room):
    fetched = [place for place, kind in enumerate(kinds) if kind == "in"]
    given, total = len(operands), len(outs)
    held = {"in": pltpu.HBM, "hbm": pltpu.HBM, "smem": pltpu.SMEM}

    def body(*refs):
        ins, rest = list(refs[:given]), refs[given:]
        made, rest = rest[:total], rest[total:]
        buffers, arrived = rest[: len(fetched)], rest[len(fetched)]
        copies = []
        for index, place in enumerate(fetched):
            copies.append(
                pltpu.make_async_copy(ins[place], buffers[index], arrived.at[index])
            )
            copies[-1].start()
            ins[place] = buffers[index]
        for copy in copies:
            copy.wait()
        kernel(*ins, *made, *rest[len(fetched) + 1 :])

    return pl.pallas_call(
        body,
        grid=(1,),
        out_shape=tuple(out for out, kind in outs),
        in_specs=[pl.BlockSpec(memory_space=held[kind]) for kind in kinds],
        out_specs=tuple(
            whole(out) if kind == "out" else pl.BlockSpec(memory_space=pltpu.HBM)
            for out, kind in outs
        ),
        scratch_shapes=[pltpu.VMEM(operands[place].shape, operands[place].dtype) for place in fetched]
        + [pltpu.SemaphoreType.DMA((len(fetched),))]
        + list(scratch),
        compiler_params=pltpu.CompilerParams(vmem_limit_bytes=room * 1024 * 1024),
        cost_estimate=busy(cost),
        name=name,
    )(*operands)


def to_rows(rows_ref, block, group, groups):
    rows_ref[pl.ds(group, block.shape[0], stride=groups), :] = block


def forward_kernel(
    signal_ref, delta_ref, gate_ref, inmap_ref, outmap_ref, rates_ref, skip_ref, start_ref,
    kept_ref, step_rows, signal_rows, act_ref, slope_ref, maps_ref,
    rate_rows, state_rows, out_rows, kept_rows, copied,
):
    channels, tokens = signal_ref.shape
    count = rates_ref.shape[0]
    groups = channels // LANES
    span = tokens // CHUNKS
    for g in range(groups):
        part = slice(g * LANES, (g + 1) * LANES)
        to_rows(signal_rows, signal_ref[part, :].astype(jnp.float32).T, g, groups)
        to_rows(step_rows, jax.nn.softplus(delta_ref[part, :].astype(jnp.float32)).T, g, groups)
        to_rows(rate_rows, jnp.exp(rates_ref[:, part]) * (-1.0 / LN2), g, groups)
        to_rows(state_rows, start_ref[:, part], g, groups)
    skip = skip_ref[...]

    def row(ref, index):
        return ref[pl.ds(pl.multiple_of(index * groups, groups), groups), :]

    def advance(t, carry):
        states, weighed, total = carry
        step = row(step_rows, t)
        signal = row(signal_rows, t)
        drive = step * signal
        out = skip * signal
        new_states, new_weighed = [], []
        for n in range(count):
            decay = jnp.exp2(step * rate_rows[n * groups : (n + 1) * groups, :])
            kept = decay * states[n]
            paced = step * kept
            kept_rows[t, n] = paced
            state = kept + inmap_ref[n, t] * drive
            out = out + outmap_ref[n, t] * state
            new_weighed.append(decay * weighed[n] + paced)
            new_states.append(state)
        out_rows[pl.ds(pl.multiple_of(t * groups, groups), groups), :] = out
        return (tuple(new_states), tuple(new_weighed), total + step)

    zero = jnp.zeros((groups, LANES), jnp.float32)
    first = tuple(state_rows[n * groups : (n + 1) * groups, :] for n in range(count))
    carry = (first, (zero,) * count, zero)
    copies = []
    for chunk in range(CHUNKS):
        low = chunk * span
        carry = lax.fori_loop(low, low + span, advance, carry, unroll=8)
        part = pl.ds(low, span)
        copies.append(
            pltpu.make_async_copy(kept_rows.at[part], kept_ref.at[part], copied.at[chunk])
        )
        copies[-1].start()
    unused, weighed, total = carry
    for n in range(count):
        maps_ref[n] = jnp.exp2(total * rate_rows[n * groups : (n + 1) * groups, :])
        maps_ref[count + n] = weighed[n]
    for g in range(groups):
        part = slice(g * LANES, (g + 1) * LANES)
        scan_out = out_rows[pl.ds(g, tokens, stride=groups), :].T
        gate = gate_ref[part, :].astype(jnp.float32)
        sig = jax.nn.sigmoid(gate)
        act_ref[part, :] = gate * sig
        slope_ref[part, :] = scan_out * sig * (1.0 + gate * (1.0 - sig))
    for copy in copies:
        copy.wait()


def forward_call(scan_input, delta_raw, gate_branch, state_input, state_output, log_rates, skip, start):
    channels, tokens = scan_input.shape
    count = log_rates.shape[0]
    groups = channels // LANES
    f32 = jnp.float32
    kept = pltpu.HBM((tokens, count, groups, LANES), f32)
    rows = pltpu.HBM((tokens * groups, LANES), f32)
    column = pltpu.HBM((channels, tokens), f32)
    maps = jax.ShapeDtypeStruct((2 * count, groups, LANES), f32)
    return staged_call(
        forward_kernel,
        (scan_input, delta_raw, gate_branch, state_input, state_output, log_rates, skip, start),
        ("in", "in", "in", "smem", "smem", "in", "in", "in"),
        ((kept, "hbm"),) + tuple((out, "out") for out in (rows, rows, column, column, maps)),
        [
            pltpu.VMEM((count * groups, LANES), f32),
            pltpu.VMEM((count * groups, LANES), f32),
            pltpu.VMEM((tokens * groups, LANES), f32),
            pltpu.VMEM(kept.shape, f32),
            pltpu.SemaphoreType.DMA((CHUNKS,)),
        ],
        7,
        "scan_forward",
        50,
    )


def fetch_back(kept_ref, kept_rows, copied, span):
    copies = []
    for chunk in reversed(range(CHUNKS)):
        part = pl.ds(chunk * span, span)
        copies.append(
            pltpu.make_async_copy(kept_ref.at[part], kept_rows.at[part], copied.at[chunk])
        )
        copies[-1].start()
    return copies


def local_kernel(
    extra, act_ref, slope_ref, step_rows, signal_rows, kept_ref, outmap_ref, rates_ref, *refs
):
    *inner_refs, gate_out, y_rows, sums_ref, rate_rows, kept_rows, copied = refs[extra:]
    channels, tokens = act_ref.shape
    count = rates_ref.shape[0]
    groups = channels // LANES
    span = tokens // CHUNKS
    copies = fetch_back(kept_ref, kept_rows, copied, span)
    for g in range(groups):
        part = slice(g * LANES, (g + 1) * LANES)
        inner = sum(ref[part, :].astype(jnp.float32) for ref in inner_refs)
        gate_out[part, :] = (inner * slope_ref[part, :]).astype(gate_out.dtype)
        to_rows(y_rows, (inner * act_ref[part, :]).T, g, groups)
        to_rows(rate_rows, jnp.exp(rates_ref[:, part]) * (-1.0 / LN2), g, groups)

    def row(ref, index):
        return ref[pl.ds(pl.multiple_of(index * groups, groups), groups), :]

    def advance(turn, carry):
        terms, moments, skips = carry
        t = tokens - 1 - turn
        step = row(step_rows, t)
        y_grad = row(y_rows, t)
        new_terms, new_moments = [], []
        for n in range(count):
            adjoint = outmap_ref[n, t] * y_grad + terms[n]
            new_moments.append(moments[n] + adjoint * kept_rows[t, n])
            new_terms.append(
                jnp.exp2(step * rate_rows[n * groups : (n + 1) * groups, :]) * adjoint
            )
        return (tuple(new_terms), tuple(new_moments), skips + y_grad * row(signal_rows, t))

    zero = jnp.zeros((groups, LANES), jnp.float32)
    carry = ((zero,) * count, (zero,) * count, zero)
    for turn, copy in enumerate(copies):
        copy.wait()
        carry = lax.fori_loop(turn * span, (turn + 1) * span, advance, carry, unroll=8)
    terms, moments, skips = carry
    for n in range(count):
        sums_ref[n] = terms[n]
        sums_ref[count + n] = moments[n]
    sums_ref[2 * count] = skips


def local_call(inner, joined, act, slope, steps, signals, kept, state_output, log_rates):
    channels, tokens = act.shape
    count = log_rates.shape[0]
    groups = channels // LANES
    f32 = jnp.float32
    outs = (
        jax.ShapeDtypeStruct((channels, tokens), jnp.bfloat16),
        jax.ShapeDtypeStruct((tokens * groups, LANES), f32),
        jax.ShapeDtypeStruct((2 * count + 1, groups, LANES), f32),
    )
    return staged_call(
        functools.partial(local_kernel, len(joined)),
        (act, slope, steps, signals, kept, state_output, log_rates) + tuple(joined) + tuple(inner),
        ("in", "in", "in", "in", "hbm", "smem", "in")
        + ("hbm",) * len(joined)
        + ("in",) * len(inner),
        tuple((out, "out") for out in outs),
        [
            pltpu.VMEM((count * groups, LANES), f32),
            pltpu.VMEM(kept.shape, f32),
            pltpu.SemaphoreType.DMA((CHUNKS,)),
        ],
        6,
        "scan_local",
        50,
    )


def adjoint_kernel(
    incoming_ref, y_rows, step_rows, signal_rows, kept_ref, delta_ref, inmap_ref, outmap_ref,
    rates_ref, skip_ref,
    input_out, delta_out,
    rate_rows, in_rows, slope_rows, kept_rows, copied,
):
    channels, tokens = delta_ref.shape
    count = rates_ref.shape[0]
    groups = channels // LANES
    span = tokens // CHUNKS
    copies = fetch_back(kept_ref, kept_rows, copied, span)
    for g in range(groups):
        part = slice(g * LANES, (g + 1) * LANES)
        to_rows(rate_rows, jnp.exp(rates_ref[:, part]) * (-1.0 / LN2), g, groups)
    skip = skip_ref[...]

    def row(ref, index):
        return ref[pl.ds(pl.multiple_of(index * groups, groups), groups), :]

    def advance(turn, later):
        t = tokens - 1 - turn
        step = row(step_rows, t)
        y_grad = row(y_rows, t)
        pulled = jnp.zeros((groups, LANES), jnp.float32)
        decayed = jnp.zeros((groups, LANES), jnp.float32)
        new_later = []
        for n in range(count):
            rate = rate_rows[n * groups : (n + 1) * groups, :]
            adjoint = outmap_ref[n, t] * y_grad + later[n]
            pulled = pulled + inmap_ref[n, t] * adjoint
            decayed = decayed + adjoint * kept_rows[t, n] * rate
            new_later.append(jnp.exp2(step * rate) * adjoint)
        here = pl.ds(pl.multiple_of(t * groups, groups), groups)
        in_rows[here, :] = pulled * step + skip * y_grad
        slope_rows[here, :] = pulled * row(signal_rows, t) + decayed * (LN2 / step)
        return tuple(new_later)

    later = tuple(incoming_ref[n] for n in range(count))
    for turn, copy in enumerate(copies):
        copy.wait()
        later = lax.fori_loop(turn * span, (turn + 1) * span, advance, later, unroll=8)
    for g in range(groups):
        part = slice(g * LANES, (g + 1) * LANES)
        input_out[part, :] = in_rows[pl.ds(g, tokens, stride=groups), :].T.astype(input_out.dtype)
        sig = jax.nn.sigmoid(delta_ref[part, :].astype(jnp.float32))
        slope = slope_rows[pl.ds(g, tokens, stride=groups), :].T
        delta_out[part, :] = (slope * sig).astype(delta_out.dtype)


def adjoint_call(incoming, y_grads, steps, signals, kept, delta_raw, state_input, state_output, log_rates, skip):
    channels, tokens = delta_raw.shape
    count = log_rates.shape[0]
    groups = channels // LANES
    f32 = jnp.float32
    out = jax.ShapeDtypeStruct((channels, tokens), jnp.bfloat16)
    return staged_call(
        adjoint_kernel,
        (incoming, y_grads, steps, signals, kept, delta_raw, state_input, state_output, log_rates, skip),
        ("in", "in", "in", "in", "hbm", "in", "smem", "smem", "in", "in"),
        ((out, "out"), (out, "out")),
        [
            pltpu.VMEM((count * groups, LANES), f32),
            pltpu.VMEM((tokens * groups, LANES), f32),
            pltpu.VMEM((tokens * groups, LANES), f32),
            pltpu.VMEM(kept.shape, f32),
            pltpu.SemaphoreType.DMA((CHUNKS,)),
        ],
        7,
        "scan_adjoint",
        50,
    )


def swap(value, axis, distance=1):
    count = lax.axis_size(axis)
    return lax.ppermute(value, axis, [(place, place ^ distance) for place in range(count)])


def full_spec(shape):
    return pl.BlockSpec(shape, lambda *unused: (0,) * len(shape))


def marks_rows(experts):
    return -(-(2 * experts + 2) // 8) * 8


def route_kernel(low, high, places_ref, ids_ref, gains_ref, input_ref, grad_ref, *refs):
    outs = refs[: high - low]
    tokens = input_ref.shape[0]
    capacity = outs[0].shape[1]
    experts = (places_ref.shape[0] - 2) // 3
    place = places_ref[3 * experts]
    wanted = lax.broadcasted_iota(jnp.int32, (experts, tokens), 0) ^ place
    first, second = ids_ref[0:1, :] == wanted, ids_ref[1:2, :] == wanted
    hits = first | second
    before = lax.broadcasted_iota(jnp.int32, (tokens, tokens), 0) < lax.broadcasted_iota(
        jnp.int32, (tokens, tokens), 1
    )
    slots = jnp.dot(
        hits.astype(jnp.float32).astype(jnp.bfloat16),
        before.astype(jnp.float32).astype(jnp.bfloat16),
        preferred_element_type=jnp.float32,
    )
    slots = jnp.where(hits, slots, -1.0)
    lines = lax.broadcasted_iota(jnp.int32, (capacity, tokens), 0).astype(jnp.float32)
    for d in range(low, high):
        chosen = jnp.where(slots[d : d + 1, :] == lines, 1.0, 0.0).astype(jnp.bfloat16)
        for index, source in enumerate((input_ref, grad_ref)):
            outs[d - low][index] = jnp.dot(
                chosen, source[...], preferred_element_type=jnp.float32
            ).astype(jnp.bfloat16)
    if low:
        return
    marks_ref, mark_rows = refs[-2:]
    mark_rows[...] = jnp.zeros_like(mark_rows)
    mark_rows[0:experts, :] = slots
    mark_rows[experts : 2 * experts, :] = jnp.where(
        first, gains_ref[0:1, :], jnp.where(second, gains_ref[1:2, :], 0.0)
    )
    mark_rows[2 * experts : 2 * experts + 2, :] = ids_ref[...].astype(jnp.float32)
    marks_ref[...] = mark_rows[...].T


def route_call(places, ids, gains, moe_input, out_grad, experts, capacity):
    tokens, feats = moe_input.shape
    out = jax.ShapeDtypeStruct((2, capacity, feats), jnp.bfloat16)
    lines = marks_rows(experts)
    marks = jax.ShapeDtypeStruct((tokens, lines), jnp.float32)
    given = (places, ids.T, gains.T, moe_input, out_grad)
    kinds = ("smem", "in", "in", "in", "in")
    far = staged_call(
        functools.partial(route_kernel, 1, experts), given, kinds, ((out, "out"),) * (experts - 1),
        [], 1, "route_rows", 63,
    )
    own, marks = staged_call(
        lambda *refs: route_kernel(0, 1, *refs[:5], *refs[6:]),
        given + (far[0],),
        kinds + ("hbm",),
        ((out, "out"), (marks, "out")),
        [pltpu.VMEM((lines, tokens), jnp.float32)],
        1,
        "route_own",
        63,
    )
    return (own,) + tuple(far), marks


def follow(value, *after):
    anywhere = pl.BlockSpec(memory_space=pl.ANY)
    return pl.pallas_call(
        lambda *refs: None,
        out_shape=jax.ShapeDtypeStruct(value.shape, value.dtype),
        in_specs=[anywhere] * (1 + len(after)),
        out_specs=anywhere,
        input_output_aliases={0: 0},
        name="follow",
    )(value, *after)


def spread_plane(rows, crosswise):
    row_count = lax.axis_size("row")
    across = swap(rows, "half")
    beside = [swap(rows, "row", r) for r in range(1, row_count)]
    if crosswise:
        corner = [swap(across, "row", r) for r in range(1, row_count)]
    else:
        corner = [swap(part, "half") for part in beside]
    mine = [rows, across] + beside + corner
    near = swap(jnp.stack(mine[: 1 + row_count]), "core")
    return mine + [near] + [swap(part, "core") for part in corner]


def piece_of(refs, row_count, core, row, half):
    if core == 0:
        return refs[half if row == 0 else half * (row_count - 1) + 1 + row]
    if row and half:
        return refs[2 * row_count + row]
    return refs[2 * row_count].at[half if row == 0 else 1 + row]


def gather_kernel(groups, blocks, first, last, places_ref, after_ref, *refs):
    row_count = blocks // 2
    per = 3 * row_count
    pieces = refs[: groups * per]
    refs = refs[groups * per :]
    weights = refs[: groups * 3]
    refs = refs[groups * 3 :]
    if not first:
        held, refs = refs[:3], refs[3:]
    outs, (rows_ref,) = refs[:-1], refs[-1:]
    unused, capacity, feats = pieces[0].shape

    @pl.when(pl.program_id(0) == 0)
    def assemble():
        half = places_ref[places_ref.shape[0] - 1]
        for q in range(groups):
            for h in range(2):
                columns = pl.ds(pl.multiple_of((half ^ h) * feats, feats), feats)
                for b in range(blocks):
                    part = piece_of(
                        pieces[q * per : (q + 1) * per], row_count, b // row_count, b % row_count, h
                    )
                    for kind in range(2):
                        rows_ref[q, kind, b * capacity : (b + 1) * capacity, columns] = part[kind]

    if first:
        gate_pre = up_pre = hidden = 0.0
    else:
        gate_pre, up_pre, hidden = (ref[...] for ref in held)
    for q in range(groups):
        gate_ref, up_ref, down_ref = weights[q * 3 : q * 3 + 3]
        rows_in, rows_grad = rows_ref[q, 0], rows_ref[q, 1]
        gate_pre += jnp.dot(rows_in, gate_ref[...], preferred_element_type=jnp.float32)
        up_pre += jnp.dot(rows_in, up_ref[...], preferred_element_type=jnp.float32)
        hidden += lax.dot_general(
            rows_grad, down_ref[...], (((1,), (1,)), ((), ())),
            preferred_element_type=jnp.float32,
        )
    if not last:
        for ref, value in zip(outs, (gate_pre, up_pre, hidden)):
            ref[...] = value
        return
    gate_out, up_out, probe_out = outs
    sig = jax.nn.sigmoid(gate_pre)
    silu = gate_pre * sig
    up_out[...] = (hidden * silu).astype(jnp.bfloat16)
    weighted = hidden * up_pre
    gate_out[...] = (weighted * sig * (1.0 + gate_pre * (1.0 - sig))).astype(jnp.bfloat16)
    probe = weighted * silu
    folded = sum(
        probe[:, at : at + LANES] for at in range(0, probe.shape[1], LANES)
    )

    @pl.when(pl.program_id(0) == 0)
    def begin():
        probe_out[...] = folded

    @pl.when(pl.program_id(0) != 0)
    def add():
        probe_out[...] += folded


def gather_call(places, distances, after, pieces, gate_weight, up_weight, down_weight, held, last):
    groups, blocks = len(pieces), 2 * lax.axis_size("row")
    unused, capacity, feats = pieces[0][0].shape
    hidden = gate_weight.shape[2]
    width = min(256, hidden)
    rows = blocks * capacity
    first = held is None
    flat = [part for q in pieces for part in q]
    in_specs = [pl.BlockSpec(memory_space=pl.ANY)]
    in_specs += [full_spec(part.shape) for part in flat]
    weights = []
    for q in distances:
        in_specs += [
            pl.BlockSpec((None, 2 * feats, width), lambda j, at, q=q: (0, at[q], j)),
            pl.BlockSpec((None, 2 * feats, width), lambda j, at, q=q: (0, at[q], j)),
            pl.BlockSpec((None, width, 2 * feats), lambda j, at, q=q: (0, j, at[q])),
        ]
        weights += [gate_weight, up_weight, down_weight]
    column = pl.BlockSpec((rows, width), lambda j, at: (0, j))
    operands = [places, after] + flat + weights
    aliases = {}
    if not first:
        if not last:
            aliases = {len(operands) + i: i for i in range(3)}
        operands += list(held)
        in_specs += [column] * 3
    if last:
        out_shape = (
            jax.ShapeDtypeStruct((rows, hidden), jnp.bfloat16),
            jax.ShapeDtypeStruct((rows, hidden), jnp.bfloat16),
            jax.ShapeDtypeStruct((rows, LANES), jnp.float32),
        )
        out_specs = (column, column, full_spec((rows, LANES)))
    else:
        out_shape = (jax.ShapeDtypeStruct((rows, hidden), jnp.float32),) * 3
        out_specs = (column,) * 3
    return pl.pallas_call(
        functools.partial(gather_kernel, groups, blocks, first, last),
        out_shape=out_shape,
        grid_spec=pltpu.PrefetchScalarGridSpec(
            num_scalar_prefetch=1,
            grid=(hidden // width,),
            in_specs=in_specs,
            out_specs=out_specs,
            scratch_shapes=[pltpu.VMEM((groups, 2, rows, 2 * feats), jnp.bfloat16)],
        ),
        input_output_aliases=aliases,
        compiler_params=pltpu.CompilerParams(vmem_limit_bytes=ROOM),
        cost_estimate=busy(4 * groups),
        name="hidden_rows",
    )(*operands)


def return_kernel(
    blocks, places_ref, gate_ref, up_ref, gate_weight, up_weight, after_ref, keep_ref, send_ref
):
    contract = (((1,), (1,)), ((), ()))
    value = lax.dot_general(
        gate_ref[...], gate_weight[...], contract, preferred_element_type=jnp.float32
    ) + lax.dot_general(up_ref[...], up_weight[...], contract, preferred_element_type=jnp.float32)
    capacity = keep_ref.shape[1]
    for b in range(blocks):
        keep_ref[b] = value[b * capacity : (b + 1) * capacity]
        at = (blocks + b) * capacity
        send_ref[b] = value[at : at + capacity].astype(jnp.bfloat16)


def return_call(places, low, high, grad_gate, grad_up, gate_weight, up_weight, after, feats, row_count):
    rows, hidden = grad_gate.shape
    count, experts = high - low, lax.axis_size("expert")
    capacity = rows // (2 * row_count)
    every = pl.BlockSpec((rows, hidden), lambda q, h, at: (0, 0))
    weight = pl.BlockSpec((None, feats, hidden), lambda q, h, at: (0, at[experts * (1 + h) + low + q], 0))
    out = pl.BlockSpec((row_count, None, None, capacity, feats), lambda q, h, at: (0, h, q, 0, 0))
    shape = (row_count, 2, count, capacity, feats)
    return pl.pallas_call(
        functools.partial(return_kernel, row_count),
        out_shape=(
            jax.ShapeDtypeStruct(shape, jnp.float32),
            jax.ShapeDtypeStruct(shape, jnp.bfloat16),
        ),
        grid_spec=pltpu.PrefetchScalarGridSpec(
            num_scalar_prefetch=1,
            grid=(count, 2),
            in_specs=[every, every, weight, weight, pl.BlockSpec(memory_space=pl.ANY)],
            out_specs=(out, out),
        ),
        compiler_params=pltpu.CompilerParams(vmem_limit_bytes=ROOM),
        cost_estimate=busy(4 * count),
        name="route_grads",
    )(places, grad_gate, grad_up, gate_weight, up_weight, after)


def corner_swap(value, distance):
    rows = lax.axis_size("row")
    pairs = [
        (row * 2 + half, (row ^ distance) * 2 + (half ^ 1))
        for row in range(rows)
        for half in range(2)
    ]
    return lax.ppermute(value, ("row", "half"), pairs)


def sum_plane(keep, send):
    row_count = keep.shape[0]
    wide, narrow = jnp.float32, jnp.bfloat16
    paired = keep + swap(send, "core").astype(wide)
    small = paired.astype(narrow)
    parts = [swap(small[0, 1], "half")]
    for r in range(1, row_count):
        parts += [corner_swap(small[r, 1], r), swap(small[r, 0], "row", r)]
    total = paired[0, 0] + sum(part.astype(wide) for part in parts)
    return small, total.astype(narrow)


def resid_kernel(marks_ref, grad_ref, *refs):
    *parts, out_ref = refs
    tokens = grad_ref.shape[0]
    experts, capacity = len(parts), parts[0].shape[0]
    lines = lax.broadcasted_iota(jnp.int32, (tokens, capacity), 1).astype(jnp.float32)
    total = grad_ref[...].astype(jnp.float32)
    for d, part in enumerate(parts):
        chosen = jnp.where(marks_ref[:, d : d + 1] == lines, 1.0, 0.0).astype(jnp.bfloat16)
        gain = marks_ref[:, experts + d : experts + d + 1]
        total += gain * jnp.dot(chosen, part[...], preferred_element_type=jnp.float32)
    out_ref[...] = total.astype(out_ref.dtype)


def resid_call(marks, out_grad, parts):
    out = jax.ShapeDtypeStruct(out_grad.shape, jnp.bfloat16)
    return staged_call(
        resid_kernel,
        (marks, out_grad) + tuple(parts),
        ("in", "in") + ("in",) * len(parts),
        ((out, "out"),),
        [],
        2,
        "resid_rows",
        44,
    )[0]


def probe_lines_kernel(probes_ref, after_ref, out_ref):
    blocks, capacity = out_ref.shape
    for b in range(blocks):
        part = probes_ref[b * capacity : (b + 1) * capacity, :].T
        out_ref[b : b + 1, :] = jnp.sum(part, axis=0, keepdims=True)


def probe_lines_call(probes, after, blocks):
    out = jax.ShapeDtypeStruct((blocks, probes.shape[0] // blocks), jnp.float32)
    return staged_call(
        probe_lines_kernel, (probes, after), ("in", "hbm"), ((out, "out"),), [], 1, "probe_lines", 16
    )[0]


def probe_kernel(places_ref, marks_ref, table_ref, out_ref):
    experts, capacity = table_ref.shape
    tokens = marks_ref.shape[0]
    place = places_ref[3 * experts]
    lines = lax.broadcasted_iota(jnp.int32, (tokens, capacity), 1).astype(jnp.float32)
    columns = lax.broadcasted_iota(jnp.int32, (tokens, 2), 1)
    named = marks_ref[:, 2 * experts : 2 * experts + 2]
    total = jnp.zeros(columns.shape, jnp.float32)
    for d in range(experts):
        taken = jnp.where(marks_ref[:, d : d + 1] == lines, table_ref[d : d + 1, :], 0.0)
        value = jnp.sum(taken, axis=1, keepdims=True)
        total += jnp.where(named == (place ^ d).astype(jnp.float32), value, 0.0)
    out_ref[...] = total


def probe_call(places, marks, table):
    out = jax.ShapeDtypeStruct((marks.shape[0], 2), jnp.float32)
    return staged_call(
        probe_kernel, (places, marks, table), ("smem", "in", "in"), ((out, "out"),), [], 1,
        "probe_rows",
        16,
    )[0]


def project_kernel(places_ref, far_weight, own_weight, resid_ref, after_ref, far_ref, own_ref):
    for weight_ref, out_ref in ((far_weight, far_ref), (own_weight, own_ref)):
        value = lax.dot_general(
            weight_ref[...], resid_ref[...], (((1,), (1,)), ((), ())),
            preferred_element_type=jnp.float32,
        )
        out_ref[...] = value.astype(out_ref.dtype)


def project_call(places, distance, out_weight, resid, after, channels):
    tokens, feats = resid.shape
    shape = (channels, tokens)
    experts = lax.axis_size("expert")
    return pl.pallas_call(
        project_kernel,
        out_shape=(
            jax.ShapeDtypeStruct(shape, jnp.bfloat16),
            jax.ShapeDtypeStruct(shape, jnp.float32),
        ),
        grid_spec=pltpu.PrefetchScalarGridSpec(
            num_scalar_prefetch=1,
            grid=(1,),
            in_specs=[
                pl.BlockSpec((channels, feats), lambda i, at: (at[2 * experts + distance], 0)),
                pl.BlockSpec((channels, feats), lambda i, at: (at[experts + distance], 0)),
                full_spec((tokens, feats)),
                pl.BlockSpec(memory_space=pl.ANY),
            ],
            out_specs=(full_spec(shape),) * 2,
        ),
        compiler_params=pltpu.CompilerParams(vmem_limit_bytes=ROOM),
        cost_estimate=busy(2),
        name="inner_parts",
    )(places, out_weight, out_weight, resid, after)


def probe_table(lines):
    experts, rows = lax.axis_size("expert"), lax.axis_size("row")
    lines = lines.reshape(2, rows, lines.shape[1])
    lines = lines[0] + swap(lines[1], "core")
    lines = lines[0] + sum(swap(lines[r], "row", r) for r in range(1, rows))
    lines = lines + swap(lines, "half")
    return jnp.stack([lines] + [swap(lines, "expert", d) for d in range(1, experts)])


def in_order(own, other):
    first = lax.axis_index("core") == 0
    return jnp.where(first, own, other), jnp.where(first, other, own)


def join_maps(maps):
    count = maps.shape[0] // 2
    former, latter = in_order(maps, swap(maps, "core"))
    decay = former[:count] * latter[:count]
    weight = latter[count:] + former[count:] * latter[:count]
    joined = jnp.concatenate([decay, weight], axis=0)
    rows = lax.axis_size("row")
    return former, latter, [joined] + [swap(joined, "row", r) for r in range(1, rows)]


def join_sums(sums, former, latter, joined):
    count = joined[0].shape[0] // 2
    rows, row = lax.axis_size("row"), lax.axis_index("row")
    ahead, behind = in_order(sums, swap(sums, "core"))
    own_term = behind[:count]
    both = ahead + behind
    pair = jnp.concatenate(
        [
            ahead[:count] + former[:count] * own_term,
            both[count : 2 * count] + former[count:] * own_term,
            both[2 * count :],
        ],
        axis=0,
    )
    pairs = [pair] + [swap(pair, "row", r) for r in range(1, rows)]
    carried = jnp.zeros_like(own_term)
    incoming = jnp.zeros_like(own_term)
    moment = jnp.zeros_like(own_term)
    for place in reversed(range(rows)):
        maps_here, pair_here = joined[0], pair
        for r in range(1, rows):
            there = (row ^ r) == place
            maps_here = jnp.where(there, joined[r], maps_here)
            pair_here = jnp.where(there, pairs[r], pair_here)
        incoming = jnp.where(row == place, carried, incoming)
        moment = moment + pair_here[count : 2 * count] + maps_here[count:] * carried
        carried = pair_here[:count] + maps_here[:count] * carried
    skips = sum(part[2 * count] for part in pairs)
    into_first = own_term + latter[:count] * incoming
    return jnp.where(lax.axis_index("core") == 0, into_first, incoming), moment, skips


def local(
    moe_input,
    out_grad,
    expert_ids,
    expert_route_weights,
    gate_weight,
    up_weight,
    down_weight,
    out_weight,
    scan_input,
    delta_raw,
    mixer_gate_branch,
    state_input,
    state_output,
    log_rates,
    skip_gain,
    block_states,
):
    experts = lax.axis_size("expert")
    row_count = lax.axis_size("row")
    tokens, feats = moe_input.shape
    capacity = 3 * expert_ids.shape[1] * tokens // (2 * experts)
    channels = scan_input.shape[0]
    groups = channels // LANES
    states = log_rates.shape[0]
    skip_rows = skip_gain.reshape(groups, LANES)
    apart = np.arange(experts) ^ np.arange(experts)[:, None]
    table = np.zeros((experts, 2, 3 * experts + 2), np.int32)
    for half in range(2):
        table[:, half, :experts] = apart
        table[:, half, experts : 2 * experts] = 2 * apart + half
        table[:, half, 2 * experts : 3 * experts] = 2 * apart + 1 - half
        table[:, half, 3 * experts] = np.arange(experts)
        table[:, half, 3 * experts + 1] = half
    places = lax.dynamic_index_in_dim(
        jnp.asarray(table.reshape(2 * experts, -1)),
        2 * lax.axis_index("expert") + lax.axis_index("half"),
        keepdims=False,
    )

    kept, steps, signals, act, slope, maps = forward_call(
        scan_input, delta_raw, mixer_gate_branch, state_input, state_output, log_rates, skip_rows,
        block_states[0],
    )
    sent, marks = route_call(
        places, expert_ids, expert_route_weights, moe_input, out_grad, experts, capacity
    )
    got = {}
    for d in ORDER:
        got[d] = sent[d] if d == 0 else swap(sent[d], "expert", d)
        if d == 1:
            got[d] = follow(got[d], maps)
    held = None
    queue = []
    step = 0
    for index, d in enumerate(ORDER):
        queue.append((d, spread_plane(got[d], d % 2 == 0)))
        while step < len(PLAN) and PLAN[step][0] == index:
            took = PLAN[step][1]
            group, queue = queue[:took], queue[took:]
            step += 1
            held = gather_call(
                places,
                [q for q, unused in group],
                maps,
                [pieces for unused, pieces in group],
                gate_weight, up_weight, down_weight, held, step == len(PLAN),
            )
    grad_gate, grad_up, probes = held

    parts = [None] * experts
    after = [probes] * LAG
    for low, high in GROUPS:
        low, high = low * experts // 4, high * experts // 4
        keep, send = return_call(
            places, low, high, grad_gate, grad_up, gate_weight, up_weight, after[-LAG], feats,
            row_count,
        )
        small, summed = sum_plane(keep, send)
        after.append(small)
        for d in reversed(range(low, high)):
            parts[d] = summed[d - low] if d == 0 else swap(summed[d - low], "expert", d)
    resid_grad = resid_call(marks, out_grad, parts)
    lines = probe_lines_call(probes, grad_up, 2 * row_count)
    probs_grad = probe_call(places, marks, probe_table(lines))

    inner = [None] * experts
    after = resid_grad
    for d in reversed(range(experts)):
        far_part, own_part = project_call(
            places, d, out_weight, resid_grad, after, channels
        )
        after = far_part
        total = own_part + swap(far_part, "half").astype(jnp.float32)
        inner[d] = total if d == 0 else swap(total.astype(jnp.bfloat16), "expert", d)

    former, latter, joined = join_maps(maps)
    gate_grad, y_grads, sums = local_call(
        inner, joined, act, slope, steps, signals, kept, state_output, log_rates
    )
    incoming, moment, skips = join_sums(sums, former, latter, joined)
    input_grad, delta_grad = adjoint_call(
        incoming, y_grads, steps, signals, kept, delta_raw, state_input, state_output, log_rates,
        skip_rows,
    )
    rates_grad = -jnp.exp(log_rates) * moment.reshape(states, channels)
    skip_grad = skips.reshape(channels)
    return (resid_grad, probs_grad, input_grad, delta_grad, gate_grad, rates_grad, skip_grad)


def solution(mesh):
    seq_count, exp_count = mesh.shape["seq"], mesh.shape["exp"]
    split = Mesh(
        mesh.devices.reshape(seq_count // 2, 2, exp_count // 2, 2),
        ("row", "core", "expert", "half"),
    )
    seq, exp = ("row", "core"), ("expert", "half")
    in_specs = (
        P(seq, exp),
        P(seq, exp),
        P(seq, None),
        P(seq, None),
        P(exp, None, seq),
        P(exp, None, seq),
        P(exp, seq, None),
        P(None, exp),
        P(exp, seq),
        P(exp, seq),
        P(exp, seq),
        P(None, seq),
        P(None, seq),
        P(None, exp),
        P(exp),
        P(seq, None, exp),
    )
    out_specs = (
        P(seq, exp),
        P(seq, None),
        P(exp, seq),
        P(exp, seq),
        P(exp, seq),
        P(None, exp),
        P(exp),
    )
    return jax.shard_map(local, mesh=split, in_specs=in_specs, out_specs=out_specs, check_vma=False)
```

```python
import functools
import math

import jax
import jax.numpy as jnp
import numpy as np
from jax import lax
from jax.experimental import pallas as pl
from jax.experimental.pallas import tpu as pltpu
from jax.sharding import Mesh, PartitionSpec as P

ORDER = (0, 1, 3, 2)
PLAN = ((3, 4),)
GROUPS = ((2, 4), (0, 2))
LAG = 1
LN2 = math.log(2.0)
LANES = 128
ROOM = 44 * 1024 * 1024


CHUNKS = 8


def whole(array):
    zeros = (0,) * len(array.shape)
    return pl.BlockSpec(array.shape, lambda *unused: zeros)


def busy(microseconds):
    return pl.CostEstimate(
        flops=int(microseconds * 1.1e9 * 3.0), bytes_accessed=0, transcendentals=0
    )


def staged_call(kernel, operands, kinds, outs, scratch, cost, name, room, early=None):
    fetched = [place for place, kind in enumerate(kinds) if kind == "in"]
    given, total = len(operands), len(outs)
    held = {"in": pltpu.HBM, "hbm": pltpu.HBM, "smem": pltpu.SMEM}

    def body(*refs):
        ins, rest = list(refs[:given]), refs[given:]
        made, rest = rest[:total], rest[total:]
        buffers, arrived = rest[: len(fetched)], rest[len(fetched)]
        copies = []
        for index, place in enumerate(fetched):
            copies.append(
                pltpu.make_async_copy(ins[place], buffers[index], arrived.at[index])
            )
            copies[-1].start()
            ins[place] = buffers[index]
        if early is not None:
            first_back(ins[early], rest[-2], rest[-1]).start()
        for copy in copies:
            copy.wait()
        kernel(*ins, *made, *rest[len(fetched) + 1 :])

    return pl.pallas_call(
        body,
        grid=(1,),
        out_shape=tuple(out for out, kind in outs),
        in_specs=[pl.BlockSpec(memory_space=held[kind]) for kind in kinds],
        out_specs=tuple(
            whole(out) if kind == "out" else pl.BlockSpec(memory_space=pltpu.HBM)
            for out, kind in outs
        ),
        scratch_shapes=[pltpu.VMEM(operands[place].shape, operands[place].dtype) for place in fetched]
        + [pltpu.SemaphoreType.DMA((len(fetched),))]
        + list(scratch),
        compiler_params=pltpu.CompilerParams(vmem_limit_bytes=room * 1024 * 1024),
        cost_estimate=busy(cost),
        name=name,
    )(*operands)


def to_rows(rows_ref, block, group, groups):
    rows_ref[pl.ds(group, block.shape[0], stride=groups), :] = block


def forward_kernel(
    signal_ref, delta_ref, gate_ref, inmap_ref, outmap_ref, rates_ref, skip_ref, start_ref,
    kept_ref, step_rows, signal_rows, act_ref, slope_ref, maps_ref,
    rate_rows, state_rows, out_rows, kept_rows, copied,
):
    channels, tokens = signal_ref.shape
    count = rates_ref.shape[0]
    groups = channels // LANES
    span = tokens // CHUNKS
    for g in range(groups):
        part = slice(g * LANES, (g + 1) * LANES)
        to_rows(signal_rows, signal_ref[part, :].astype(jnp.float32).T, g, groups)
        to_rows(step_rows, jax.nn.softplus(delta_ref[part, :].astype(jnp.float32)).T, g, groups)
        to_rows(rate_rows, jnp.exp(rates_ref[:, part]) * (-1.0 / LN2), g, groups)
        to_rows(state_rows, start_ref[:, part], g, groups)
    skip = skip_ref[...]

    def row(ref, index):
        return ref[pl.ds(pl.multiple_of(index * groups, groups), groups), :]

    def advance(t, carry):
        states, weighed, total = carry
        step = row(step_rows, t)
        signal = row(signal_rows, t)
        drive = step * signal
        out = skip * signal
        new_states, new_weighed = [], []
        for n in range(count):
            decay = jnp.exp2(step * rate_rows[n * groups : (n + 1) * groups, :])
            kept = decay * states[n]
            paced = step * kept
            kept_rows[t, n] = paced
            state = kept + inmap_ref[n, t] * drive
            out = out + outmap_ref[n, t] * state
            new_weighed.append(decay * weighed[n] + paced)
            new_states.append(state)
        out_rows[pl.ds(pl.multiple_of(t * groups, groups), groups), :] = out
        return (tuple(new_states), tuple(new_weighed), total + step)

    zero = jnp.zeros((groups, LANES), jnp.float32)
    first = tuple(state_rows[n * groups : (n + 1) * groups, :] for n in range(count))
    carry = (first, (zero,) * count, zero)
    copies = []
    for chunk in range(CHUNKS):
        low = chunk * span
        carry = lax.fori_loop(low, low + span, advance, carry, unroll=8)
        part = pl.ds(low, span)
        copies.append(
            pltpu.make_async_copy(kept_rows.at[part], kept_ref.at[part], copied.at[chunk])
        )
        copies[-1].start()
    unused, weighed, total = carry
    for n in range(count):
        maps_ref[n] = jnp.exp2(total * rate_rows[n * groups : (n + 1) * groups, :])
        maps_ref[count + n] = weighed[n]
    for g in range(groups):
        part = slice(g * LANES, (g + 1) * LANES)
        scan_out = out_rows[pl.ds(g, tokens, stride=groups), :].T
        gate = gate_ref[part, :].astype(jnp.float32)
        sig = jax.nn.sigmoid(gate)
        act_ref[part, :] = gate * sig
        slope_ref[part, :] = scan_out * sig * (1.0 + gate * (1.0 - sig))
    for copy in copies:
        copy.wait()


def forward_call(scan_input, delta_raw, gate_branch, state_input, state_output, log_rates, skip, start):
    channels, tokens = scan_input.shape
    count = log_rates.shape[0]
    groups = channels // LANES
    f32 = jnp.float32
    kept = pltpu.HBM((tokens, count, groups, LANES), f32)
    rows = pltpu.HBM((tokens * groups, LANES), f32)
    column = pltpu.HBM((channels, tokens), f32)
    maps = jax.ShapeDtypeStruct((2 * count, groups, LANES), f32)
    return staged_call(
        forward_kernel,
        (scan_input, delta_raw, gate_branch, state_input, state_output, log_rates, skip, start),
        ("in", "in", "in", "smem", "smem", "in", "in", "in"),
        ((kept, "hbm"),) + tuple((out, "out") for out in (rows, rows, column, column, maps)),
        [
            pltpu.VMEM((count * groups, LANES), f32),
            pltpu.VMEM((count * groups, LANES), f32),
            pltpu.VMEM((tokens * groups, LANES), f32),
            pltpu.VMEM(kept.shape, f32),
            pltpu.SemaphoreType.DMA((CHUNKS,)),
        ],
        7,
        "scan_forward",
        50,
    )


def first_back(kept_ref, kept_rows, copied):
    span = kept_rows.shape[0] // CHUNKS
    part = pl.ds((CHUNKS - 1) * span, span)
    return pltpu.make_async_copy(kept_ref.at[part], kept_rows.at[part], copied.at[CHUNKS - 1])


def fetch_back(kept_ref, kept_rows, copied, span):
    copies = []
    for chunk in reversed(range(CHUNKS)):
        part = pl.ds(chunk * span, span)
        copies.append(
            pltpu.make_async_copy(kept_ref.at[part], kept_rows.at[part], copied.at[chunk])
        )
        if len(copies) > 1:
            copies[-1].start()
    return copies


def local_kernel(
    extra, act_ref, slope_ref, step_rows, signal_rows, kept_ref, outmap_ref, rates_ref, *refs
):
    *inner_refs, gate_out, y_rows, sums_ref, rate_rows, kept_rows, copied = refs[extra:]
    channels, tokens = act_ref.shape
    count = rates_ref.shape[0]
    groups = channels // LANES
    span = tokens // CHUNKS
    copies = fetch_back(kept_ref, kept_rows, copied, span)
    for g in range(groups):
        part = slice(g * LANES, (g + 1) * LANES)
        inner = sum(ref[part, :].astype(jnp.float32) for ref in inner_refs)
        gate_out[part, :] = (inner * slope_ref[part, :]).astype(gate_out.dtype)
        to_rows(y_rows, (inner * act_ref[part, :]).T, g, groups)
        to_rows(rate_rows, jnp.exp(rates_ref[:, part]) * (-1.0 / LN2), g, groups)

    def row(ref, index):
        return ref[pl.ds(pl.multiple_of(index * groups, groups), groups), :]

    def advance(turn, carry):
        terms, moments, skips = carry
        t = tokens - 1 - turn
        step = row(step_rows, t)
        y_grad = row(y_rows, t)
        new_terms, new_moments = [], []
        for n in range(count):
            adjoint = outmap_ref[n, t] * y_grad + terms[n]
            new_moments.append(moments[n] + adjoint * kept_rows[t, n])
            new_terms.append(
                jnp.exp2(step * rate_rows[n * groups : (n + 1) * groups, :]) * adjoint
            )
        return (tuple(new_terms), tuple(new_moments), skips + y_grad * row(signal_rows, t))

    zero = jnp.zeros((groups, LANES), jnp.float32)
    carry = ((zero,) * count, (zero,) * count, zero)
    for turn, copy in enumerate(copies):
        copy.wait()
        carry = lax.fori_loop(turn * span, (turn + 1) * span, advance, carry, unroll=8)
    terms, moments, skips = carry
    for n in range(count):
        sums_ref[n] = terms[n]
        sums_ref[count + n] = moments[n]
    sums_ref[2 * count] = skips


def local_call(inner, joined, act, slope, steps, signals, kept, state_output, log_rates):
    channels, tokens = act.shape
    count = log_rates.shape[0]
    groups = channels // LANES
    f32 = jnp.float32
    outs = (
        jax.ShapeDtypeStruct((channels, tokens), jnp.bfloat16),
        jax.ShapeDtypeStruct((tokens * groups, LANES), f32),
        jax.ShapeDtypeStruct((2 * count + 1, groups, LANES), f32),
    )
    return staged_call(
        functools.partial(local_kernel, len(joined)),
        (act, slope, steps, signals, kept, state_output, log_rates) + tuple(joined) + tuple(inner),
        ("in", "in", "in", "in", "hbm", "smem", "in")
        + ("hbm",) * len(joined)
        + ("in",) * len(inner),
        tuple((out, "out") for out in outs),
        [
            pltpu.VMEM((count * groups, LANES), f32),
            pltpu.VMEM(kept.shape, f32),
            pltpu.SemaphoreType.DMA((CHUNKS,)),
        ],
        6,
        "scan_local",
        50,
        early=4,
    )


def adjoint_kernel(
    incoming_ref, y_rows, step_rows, signal_rows, kept_ref, delta_ref, inmap_ref, outmap_ref,
    rates_ref, skip_ref,
    input_out, delta_out,
    rate_rows, in_rows, slope_rows, kept_rows, copied,
):
    channels, tokens = delta_ref.shape
    count = rates_ref.shape[0]
    groups = channels // LANES
    span = tokens // CHUNKS
    copies = fetch_back(kept_ref, kept_rows, copied, span)
    for g in range(groups):
        part = slice(g * LANES, (g + 1) * LANES)
        to_rows(rate_rows, jnp.exp(rates_ref[:, part]) * (-1.0 / LN2), g, groups)
    skip = skip_ref[...]

    def row(ref, index):
        return ref[pl.ds(pl.multiple_of(index * groups, groups), groups), :]

    def advance(turn, later):
        t = tokens - 1 - turn
        step = row(step_rows, t)
        y_grad = row(y_rows, t)
        pulled = jnp.zeros((groups, LANES), jnp.float32)
        decayed = jnp.zeros((groups, LANES), jnp.float32)
        new_later = []
        for n in range(count):
            rate = rate_rows[n * groups : (n + 1) * groups, :]
            adjoint = outmap_ref[n, t] * y_grad + later[n]
            pulled = pulled + inmap_ref[n, t] * adjoint
            decayed = decayed + adjoint * kept_rows[t, n] * rate
            new_later.append(jnp.exp2(step * rate) * adjoint)
        here = pl.ds(pl.multiple_of(t * groups, groups), groups)
        in_rows[here, :] = pulled * step + skip * y_grad
        slope_rows[here, :] = pulled * row(signal_rows, t) + decayed * (LN2 / step)
        return tuple(new_later)

    later = tuple(incoming_ref[n] for n in range(count))
    for turn, copy in enumerate(copies):
        copy.wait()
        later = lax.fori_loop(turn * span, (turn + 1) * span, advance, later, unroll=8)
    for g in range(groups):
        part = slice(g * LANES, (g + 1) * LANES)
        input_out[part, :] = in_rows[pl.ds(g, tokens, stride=groups), :].T.astype(input_out.dtype)
        sig = jax.nn.sigmoid(delta_ref[part, :].astype(jnp.float32))
        slope = slope_rows[pl.ds(g, tokens, stride=groups), :].T
        delta_out[part, :] = (slope * sig).astype(delta_out.dtype)


def adjoint_call(incoming, y_grads, steps, signals, kept, delta_raw, state_input, state_output, log_rates, skip):
    channels, tokens = delta_raw.shape
    count = log_rates.shape[0]
    groups = channels // LANES
    f32 = jnp.float32
    out = jax.ShapeDtypeStruct((channels, tokens), jnp.bfloat16)
    return staged_call(
        adjoint_kernel,
        (incoming, y_grads, steps, signals, kept, delta_raw, state_input, state_output, log_rates, skip),
        ("in", "in", "in", "in", "hbm", "in", "smem", "smem", "in", "in"),
        ((out, "out"), (out, "out")),
        [
            pltpu.VMEM((count * groups, LANES), f32),
            pltpu.VMEM((tokens * groups, LANES), f32),
            pltpu.VMEM((tokens * groups, LANES), f32),
            pltpu.VMEM(kept.shape, f32),
            pltpu.SemaphoreType.DMA((CHUNKS,)),
        ],
        7,
        "scan_adjoint",
        50,
        early=4,
    )


def swap(value, axis, distance=1):
    count = lax.axis_size(axis)
    return lax.ppermute(value, axis, [(place, place ^ distance) for place in range(count)])


def full_spec(shape):
    return pl.BlockSpec(shape, lambda *unused: (0,) * len(shape))


def marks_rows(experts):
    return -(-(2 * experts + 2) // 8) * 8


def route_kernel(low, high, places_ref, ids_ref, gains_ref, input_ref, grad_ref, *refs):
    outs = refs[: high - low]
    tokens = input_ref.shape[0]
    capacity = outs[0].shape[1]
    experts = (places_ref.shape[0] - 2) // 3
    place = places_ref[3 * experts]
    wanted = lax.broadcasted_iota(jnp.int32, (experts, tokens), 0) ^ place
    first, second = ids_ref[0:1, :] == wanted, ids_ref[1:2, :] == wanted
    hits = first | second
    before = lax.broadcasted_iota(jnp.int32, (tokens, tokens), 0) < lax.broadcasted_iota(
        jnp.int32, (tokens, tokens), 1
    )
    slots = jnp.dot(
        hits.astype(jnp.float32).astype(jnp.bfloat16),
        before.astype(jnp.float32).astype(jnp.bfloat16),
        preferred_element_type=jnp.float32,
    )
    slots = jnp.where(hits, slots, -1.0)
    lines = lax.broadcasted_iota(jnp.int32, (capacity, tokens), 0).astype(jnp.float32)
    for d in range(low, high):
        chosen = jnp.where(slots[d : d + 1, :] == lines, 1.0, 0.0).astype(jnp.bfloat16)
        for index, source in enumerate((input_ref, grad_ref)):
            outs[d - low][index] = jnp.dot(
                chosen, source[...], preferred_element_type=jnp.float32
            ).astype(jnp.bfloat16)
    if low:
        return
    marks_ref, mark_rows = refs[-2:]
    mark_rows[...] = jnp.zeros_like(mark_rows)
    mark_rows[0:experts, :] = slots
    mark_rows[experts : 2 * experts, :] = jnp.where(
        first, gains_ref[0:1, :], jnp.where(second, gains_ref[1:2, :], 0.0)
    )
    mark_rows[2 * experts : 2 * experts + 2, :] = ids_ref[...].astype(jnp.float32)
    marks_ref[...] = mark_rows[...].T


def route_call(places, ids, gains, moe_input, out_grad, experts, capacity):
    tokens, feats = moe_input.shape
    out = jax.ShapeDtypeStruct((2, capacity, feats), jnp.bfloat16)
    lines = marks_rows(experts)
    marks = jax.ShapeDtypeStruct((tokens, lines), jnp.float32)
    given = (places, ids.T, gains.T, moe_input, out_grad)
    kinds = ("smem", "in", "in", "in", "in")
    far = staged_call(
        functools.partial(route_kernel, 1, experts), given, kinds, ((out, "out"),) * (experts - 1),
        [], 1, "route_rows", 63,
    )
    own, marks = staged_call(
        lambda *refs: route_kernel(0, 1, *refs[:5], *refs[6:]),
        given + (far[0],),
        kinds + ("hbm",),
        ((out, "out"), (marks, "out")),
        [pltpu.VMEM((lines, tokens), jnp.float32)],
        1,
        "route_own",
        63,
    )
    return (own,) + tuple(far), marks


def follow(value, *after):
    anywhere = pl.BlockSpec(memory_space=pl.ANY)
    return pl.pallas_call(
        lambda *refs: None,
        out_shape=jax.ShapeDtypeStruct(value.shape, value.dtype),
        in_specs=[anywhere] * (1 + len(after)),
        out_specs=anywhere,
        input_output_aliases={0: 0},
        name="follow",
    )(value, *after)


def spread_plane(rows, crosswise):
    row_count = lax.axis_size("row")
    across = swap(rows, "half")
    beside = [swap(rows, "row", r) for r in range(1, row_count)]
    if crosswise:
        corner = [swap(across, "row", r) for r in range(1, row_count)]
    else:
        corner = [swap(part, "half") for part in beside]
    mine = [rows, across] + beside + corner
    near = swap(jnp.stack(mine[: 1 + row_count]), "core")
    return mine + [near] + [swap(part, "core") for part in corner]


def piece_of(refs, row_count, core, row, half):
    if core == 0:
        return refs[half if row == 0 else half * (row_count - 1) + 1 + row]
    if row and half:
        return refs[2 * row_count + row]
    return refs[2 * row_count].at[half if row == 0 else 1 + row]


def gather_kernel(groups, blocks, first, last, places_ref, after_ref, *refs):
    row_count = blocks // 2
    per = 3 * row_count
    pieces = refs[: groups * per]
    refs = refs[groups * per :]
    weights = refs[: groups * 3]
    refs = refs[groups * 3 :]
    if not first:
        held, refs = refs[:3], refs[3:]
    outs, (rows_ref,) = refs[:-1], refs[-1:]
    unused, capacity, feats = pieces[0].shape

    @pl.when(pl.program_id(0) == 0)
    def assemble():
        half = places_ref[places_ref.shape[0] - 1]
        for q in range(groups):
            for h in range(2):
                columns = pl.ds(pl.multiple_of((half ^ h) * feats, feats), feats)
                for b in range(blocks):
                    part = piece_of(
                        pieces[q * per : (q + 1) * per], row_count, b // row_count, b % row_count, h
                    )
                    for kind in range(2):
                        rows_ref[q, kind, b * capacity : (b + 1) * capacity, columns] = part[kind]

    if first:
        gate_pre = up_pre = hidden = 0.0
    else:
        gate_pre, up_pre, hidden = (ref[...] for ref in held)
    for q in range(groups):
        gate_ref, up_ref, down_ref = weights[q * 3 : q * 3 + 3]
        rows_in, rows_grad = rows_ref[q, 0], rows_ref[q, 1]
        gate_pre += jnp.dot(rows_in, gate_ref[...], preferred_element_type=jnp.float32)
        up_pre += jnp.dot(rows_in, up_ref[...], preferred_element_type=jnp.float32)
        hidden += lax.dot_general(
            rows_grad, down_ref[...], (((1,), (1,)), ((), ())),
            preferred_element_type=jnp.float32,
        )
    if not last:
        for ref, value in zip(outs, (gate_pre, up_pre, hidden)):
            ref[...] = value
        return
    gate_out, up_out, probe_out = outs
    sig = jax.nn.sigmoid(gate_pre)
    silu = gate_pre * sig
    up_out[...] = (hidden * silu).astype(jnp.bfloat16)
    weighted = hidden * up_pre
    gate_out[...] = (weighted * sig * (1.0 + gate_pre * (1.0 - sig))).astype(jnp.bfloat16)
    probe = weighted * silu
    folded = sum(
        probe[:, at : at + LANES] for at in range(0, probe.shape[1], LANES)
    )

    @pl.when(pl.program_id(0) == 0)
    def begin():
        probe_out[...] = folded

    @pl.when(pl.program_id(0) != 0)
    def add():
        probe_out[...] += folded


def gather_call(places, distances, after, pieces, gate_weight, up_weight, down_weight, held, last):
    groups, blocks = len(pieces), 2 * lax.axis_size("row")
    unused, capacity, feats = pieces[0][0].shape
    hidden = gate_weight.shape[2]
    width = min(256, hidden)
    rows = blocks * capacity
    first = held is None
    flat = [part for q in pieces for part in q]
    in_specs = [pl.BlockSpec(memory_space=pl.ANY)]
    in_specs += [full_spec(part.shape) for part in flat]
    weights = []
    for q in distances:
        in_specs += [
            pl.BlockSpec((None, 2 * feats, width), lambda j, at, q=q: (0, at[q], j)),
            pl.BlockSpec((None, 2 * feats, width), lambda j, at, q=q: (0, at[q], j)),
            pl.BlockSpec((None, width, 2 * feats), lambda j, at, q=q: (0, j, at[q])),
        ]
        weights += [gate_weight, up_weight, down_weight]
    column = pl.BlockSpec((rows, width), lambda j, at: (0, j))
    operands = [places, after] + flat + weights
    aliases = {}
    if not first:
        if not last:
            aliases = {len(operands) + i: i for i in range(3)}
        operands += list(held)
        in_specs += [column] * 3
    if last:
        out_shape = (
            jax.ShapeDtypeStruct((rows, hidden), jnp.bfloat16),
            jax.ShapeDtypeStruct((rows, hidden), jnp.bfloat16),
            jax.ShapeDtypeStruct((rows, LANES), jnp.float32),
        )
        out_specs = (column, column, full_spec((rows, LANES)))
    else:
        out_shape = (jax.ShapeDtypeStruct((rows, hidden), jnp.float32),) * 3
        out_specs = (column,) * 3
    return pl.pallas_call(
        functools.partial(gather_kernel, groups, blocks, first, last),
        out_shape=out_shape,
        grid_spec=pltpu.PrefetchScalarGridSpec(
            num_scalar_prefetch=1,
            grid=(hidden // width,),
            in_specs=in_specs,
            out_specs=out_specs,
            scratch_shapes=[pltpu.VMEM((groups, 2, rows, 2 * feats), jnp.bfloat16)],
        ),
        input_output_aliases=aliases,
        compiler_params=pltpu.CompilerParams(vmem_limit_bytes=ROOM),
        cost_estimate=busy(4 * groups),
        name="hidden_rows",
    )(*operands)


def return_kernel(
    blocks, places_ref, gate_ref, up_ref, gate_weight, up_weight, after_ref, keep_ref, send_ref
):
    contract = (((1,), (1,)), ((), ()))
    value = lax.dot_general(
        gate_ref[...], gate_weight[...], contract, preferred_element_type=jnp.float32
    ) + lax.dot_general(up_ref[...], up_weight[...], contract, preferred_element_type=jnp.float32)
    capacity = keep_ref.shape[1]
    for b in range(blocks):
        keep_ref[b] = value[b * capacity : (b + 1) * capacity]
        at = (blocks + b) * capacity
        send_ref[b] = value[at : at + capacity].astype(jnp.bfloat16)


def return_call(places, low, high, grad_gate, grad_up, gate_weight, up_weight, after, feats, row_count):
    rows, hidden = grad_gate.shape
    count, experts = high - low, lax.axis_size("expert")
    capacity = rows // (2 * row_count)
    every = pl.BlockSpec((rows, hidden), lambda q, h, at: (0, 0))
    weight = pl.BlockSpec((None, feats, hidden), lambda q, h, at: (0, at[experts * (1 + h) + low + q], 0))
    out = pl.BlockSpec((row_count, None, None, capacity, feats), lambda q, h, at: (0, h, q, 0, 0))
    shape = (row_count, 2, count, capacity, feats)
    return pl.pallas_call(
        functools.partial(return_kernel, row_count),
        out_shape=(
            jax.ShapeDtypeStruct(shape, jnp.float32),
            jax.ShapeDtypeStruct(shape, jnp.bfloat16),
        ),
        grid_spec=pltpu.PrefetchScalarGridSpec(
            num_scalar_prefetch=1,
            grid=(count, 2),
            in_specs=[every, every, weight, weight, pl.BlockSpec(memory_space=pl.ANY)],
            out_specs=(out, out),
        ),
        compiler_params=pltpu.CompilerParams(vmem_limit_bytes=ROOM),
        cost_estimate=busy(4 * count),
        name="route_grads",
    )(places, grad_gate, grad_up, gate_weight, up_weight, after)


def corner_swap(value, distance):
    rows = lax.axis_size("row")
    pairs = [
        (row * 2 + half, (row ^ distance) * 2 + (half ^ 1))
        for row in range(rows)
        for half in range(2)
    ]
    return lax.ppermute(value, ("row", "half"), pairs)


def sum_plane(keep, send):
    row_count = keep.shape[0]
    wide, narrow = jnp.float32, jnp.bfloat16
    paired = keep + swap(send, "core").astype(wide)
    small = paired.astype(narrow)
    parts = [swap(small[0, 1], "half")]
    for r in range(1, row_count):
        parts += [corner_swap(small[r, 1], r), swap(small[r, 0], "row", r)]
    total = paired[0, 0] + sum(part.astype(wide) for part in parts)
    return small, total.astype(narrow)


def resid_kernel(marks_ref, grad_ref, *refs):
    *parts, out_ref = refs
    tokens = grad_ref.shape[0]
    experts, capacity = len(parts), parts[0].shape[0]
    lines = lax.broadcasted_iota(jnp.int32, (tokens, capacity), 1).astype(jnp.float32)
    total = grad_ref[...].astype(jnp.float32)
    for d, part in enumerate(parts):
        chosen = jnp.where(marks_ref[:, d : d + 1] == lines, 1.0, 0.0).astype(jnp.bfloat16)
        gain = marks_ref[:, experts + d : experts + d + 1]
        total += gain * jnp.dot(chosen, part[...], preferred_element_type=jnp.float32)
    out_ref[...] = total.astype(out_ref.dtype)


def resid_call(marks, out_grad, parts):
    out = jax.ShapeDtypeStruct(out_grad.shape, jnp.bfloat16)
    return staged_call(
        resid_kernel,
        (marks, out_grad) + tuple(parts),
        ("in", "in") + ("in",) * len(parts),
        ((out, "out"),),
        [],
        2,
        "resid_rows",
        44,
    )[0]


def probe_lines_kernel(probes_ref, after_ref, out_ref):
    blocks, capacity = out_ref.shape
    for b in range(blocks):
        part = probes_ref[b * capacity : (b + 1) * capacity, :].T
        out_ref[b : b + 1, :] = jnp.sum(part, axis=0, keepdims=True)


def probe_lines_call(probes, after, blocks):
    out = jax.ShapeDtypeStruct((blocks, probes.shape[0] // blocks), jnp.float32)
    return staged_call(
        probe_lines_kernel, (probes, after), ("in", "hbm"), ((out, "out"),), [], 1, "probe_lines", 16
    )[0]


def probe_kernel(places_ref, marks_ref, table_ref, out_ref):
    experts, capacity = table_ref.shape
    tokens = marks_ref.shape[0]
    place = places_ref[3 * experts]
    lines = lax.broadcasted_iota(jnp.int32, (tokens, capacity), 1).astype(jnp.float32)
    columns = lax.broadcasted_iota(jnp.int32, (tokens, 2), 1)
    named = marks_ref[:, 2 * experts : 2 * experts + 2]
    total = jnp.zeros(columns.shape, jnp.float32)
    for d in range(experts):
        taken = jnp.where(marks_ref[:, d : d + 1] == lines, table_ref[d : d + 1, :], 0.0)
        value = jnp.sum(taken, axis=1, keepdims=True)
        total += jnp.where(named == (place ^ d).astype(jnp.float32), value, 0.0)
    out_ref[...] = total


def probe_call(places, marks, table):
    out = jax.ShapeDtypeStruct((marks.shape[0], 2), jnp.float32)
    return staged_call(
        probe_kernel, (places, marks, table), ("smem", "in", "in"), ((out, "out"),), [], 1,
        "probe_rows",
        16,
    )[0]


def project_kernel(places_ref, far_weight, own_weight, resid_ref, after_ref, far_ref, own_ref):
    for weight_ref, out_ref in ((far_weight, far_ref), (own_weight, own_ref)):
        value = lax.dot_general(
            weight_ref[...], resid_ref[...], (((1,), (1,)), ((), ())),
            preferred_element_type=jnp.float32,
        )
        out_ref[...] = value.astype(out_ref.dtype)


def project_call(places, distance, out_weight, resid, after, channels):
    tokens, feats = resid.shape
    shape = (channels, tokens)
    experts = lax.axis_size("expert")
    return pl.pallas_call(
        project_kernel,
        out_shape=(
            jax.ShapeDtypeStruct(shape, jnp.bfloat16),
            jax.ShapeDtypeStruct(shape, jnp.float32),
        ),
        grid_spec=pltpu.PrefetchScalarGridSpec(
            num_scalar_prefetch=1,
            grid=(1,),
            in_specs=[
                pl.BlockSpec((channels, feats), lambda i, at: (at[2 * experts + distance], 0)),
                pl.BlockSpec((channels, feats), lambda i, at: (at[experts + distance], 0)),
                full_spec((tokens, feats)),
                pl.BlockSpec(memory_space=pl.ANY),
            ],
            out_specs=(full_spec(shape),) * 2,
        ),
        compiler_params=pltpu.CompilerParams(vmem_limit_bytes=ROOM),
        cost_estimate=busy(2),
        name="inner_parts",
    )(places, out_weight, out_weight, resid, after)


def probe_table(lines):
    experts, rows = lax.axis_size("expert"), lax.axis_size("row")
    lines = lines.reshape(2, rows, lines.shape[1])
    lines = lines[0] + swap(lines[1], "core")
    lines = lines[0] + sum(swap(lines[r], "row", r) for r in range(1, rows))
    lines = lines + swap(lines, "half")
    return jnp.stack([lines] + [swap(lines, "expert", d) for d in range(1, experts)])


def in_order(own, other):
    first = lax.axis_index("core") == 0
    return jnp.where(first, own, other), jnp.where(first, other, own)


def join_maps(maps):
    count = maps.shape[0] // 2
    former, latter = in_order(maps, swap(maps, "core"))
    decay = former[:count] * latter[:count]
    weight = latter[count:] + former[count:] * latter[:count]
    joined = jnp.concatenate([decay, weight], axis=0)
    rows = lax.axis_size("row")
    return former, latter, [joined] + [swap(joined, "row", r) for r in range(1, rows)]


def join_sums(sums, former, latter, joined):
    count = joined[0].shape[0] // 2
    rows, row = lax.axis_size("row"), lax.axis_index("row")
    ahead, behind = in_order(sums, swap(sums, "core"))
    own_term = behind[:count]
    both = ahead + behind
    pair = jnp.concatenate(
        [
            ahead[:count] + former[:count] * own_term,
            both[count : 2 * count] + former[count:] * own_term,
            both[2 * count :],
        ],
        axis=0,
    )
    pairs = [pair] + [swap(pair, "row", r) for r in range(1, rows)]
    carried = jnp.zeros_like(own_term)
    incoming = jnp.zeros_like(own_term)
    moment = jnp.zeros_like(own_term)
    for place in reversed(range(rows)):
        maps_here, pair_here = joined[0], pair
        for r in range(1, rows):
            there = (row ^ r) == place
            maps_here = jnp.where(there, joined[r], maps_here)
            pair_here = jnp.where(there, pairs[r], pair_here)
        incoming = jnp.where(row == place, carried, incoming)
        moment = moment + pair_here[count : 2 * count] + maps_here[count:] * carried
        carried = pair_here[:count] + maps_here[:count] * carried
    skips = sum(part[2 * count] for part in pairs)
    into_first = own_term + latter[:count] * incoming
    return jnp.where(lax.axis_index("core") == 0, into_first, incoming), moment, skips


def local(
    moe_input,
    out_grad,
    expert_ids,
    expert_route_weights,
    gate_weight,
    up_weight,
    down_weight,
    out_weight,
    scan_input,
    delta_raw,
    mixer_gate_branch,
    state_input,
    state_output,
    log_rates,
    skip_gain,
    block_states,
):
    experts = lax.axis_size("expert")
    row_count = lax.axis_size("row")
    tokens, feats = moe_input.shape
    capacity = 3 * expert_ids.shape[1] * tokens // (2 * experts)
    channels = scan_input.shape[0]
    groups = channels // LANES
    states = log_rates.shape[0]
    skip_rows = skip_gain.reshape(groups, LANES)
    apart = np.arange(experts) ^ np.arange(experts)[:, None]
    table = np.zeros((experts, 2, 3 * experts + 2), np.int32)
    for half in range(2):
        table[:, half, :experts] = apart
        table[:, half, experts : 2 * experts] = 2 * apart + half
        table[:, half, 2 * experts : 3 * experts] = 2 * apart + 1 - half
        table[:, half, 3 * experts] = np.arange(experts)
        table[:, half, 3 * experts + 1] = half
    places = lax.dynamic_index_in_dim(
        jnp.asarray(table.reshape(2 * experts, -1)),
        2 * lax.axis_index("expert") + lax.axis_index("half"),
        keepdims=False,
    )

    kept, steps, signals, act, slope, maps = forward_call(
        scan_input, delta_raw, mixer_gate_branch, state_input, state_output, log_rates, skip_rows,
        block_states[0],
    )
    sent, marks = route_call(
        places, expert_ids, expert_route_weights, moe_input, out_grad, experts, capacity
    )
    got = {}
    for d in ORDER:
        got[d] = sent[d] if d == 0 else swap(sent[d], "expert", d)
        if d == 1:
            got[d] = follow(got[d], maps)
    held = None
    queue = []
    step = 0
    for index, d in enumerate(ORDER):
        queue.append((d, spread_plane(got[d], d % 2 == 0)))
        while step < len(PLAN) and PLAN[step][0] == index:
            took = PLAN[step][1]
            group, queue = queue[:took], queue[took:]
            step += 1
            held = gather_call(
                places,
                [q for q, unused in group],
                maps,
                [pieces for unused, pieces in group],
                gate_weight, up_weight, down_weight, held, step == len(PLAN),
            )
    grad_gate, grad_up, probes = held

    parts = [None] * experts
    after = [probes] * LAG
    for low, high in GROUPS:
        low, high = low * experts // 4, high * experts // 4
        keep, send = return_call(
            places, low, high, grad_gate, grad_up, gate_weight, up_weight, after[-LAG], feats,
            row_count,
        )
        small, summed = sum_plane(keep, send)
        after.append(small)
        for d in reversed(range(low, high)):
            parts[d] = summed[d - low] if d == 0 else swap(summed[d - low], "expert", d)
    resid_grad = resid_call(marks, out_grad, parts)
    lines = probe_lines_call(probes, grad_up, 2 * row_count)
    probs_grad = probe_call(places, marks, probe_table(lines))

    inner = [None] * experts
    after = resid_grad
    for d in reversed(range(experts)):
        far_part, own_part = project_call(
            places, d, out_weight, resid_grad, after, channels
        )
        after = far_part
        total = own_part + swap(far_part, "half").astype(jnp.float32)
        inner[d] = total if d == 0 else swap(total.astype(jnp.bfloat16), "expert", d)

    former, latter, joined = join_maps(maps)
    gate_grad, y_grads, sums = local_call(
        inner, joined, act, slope, steps, signals, kept, state_output, log_rates
    )
    incoming, moment, skips = join_sums(sums, former, latter, joined)
    input_grad, delta_grad = adjoint_call(
        incoming, y_grads, steps, signals, kept, delta_raw, state_input, state_output, log_rates,
        skip_rows,
    )
    rates_grad = -jnp.exp(log_rates) * moment.reshape(states, channels)
    skip_grad = skips.reshape(channels)
    return (resid_grad, probs_grad, input_grad, delta_grad, gate_grad, rates_grad, skip_grad)


def solution(mesh):
    seq_count, exp_count = mesh.shape["seq"], mesh.shape["exp"]
    split = Mesh(
        mesh.devices.reshape(seq_count // 2, 2, exp_count // 2, 2),
        ("row", "core", "expert", "half"),
    )
    seq, exp = ("row", "core"), ("expert", "half")
    in_specs = (
        P(seq, exp),
        P(seq, exp),
        P(seq, None),
        P(seq, None),
        P(exp, None, seq),
        P(exp, None, seq),
        P(exp, seq, None),
        P(None, exp),
        P(exp, seq),
        P(exp, seq),
        P(exp, seq),
        P(None, seq),
        P(None, seq),
        P(None, exp),
        P(exp),
        P(seq, None, exp),
    )
    out_specs = (
        P(seq, exp),
        P(seq, None),
        P(exp, seq),
        P(exp, seq),
        P(exp, seq),
        P(None, exp),
        P(exp),
    )
    return jax.shard_map(local, mesh=split, in_specs=in_specs, out_specs=out_specs, check_vma=False)
```
